512 devices in a mesh: expert: 32 (over x, z), head: 16 (over y, core).
Axes of the slice: x: 4, y: 8, z: 8, core: 2. Of those that a mesh axis runs over, the one named last changes fastest.
Arguments:
- queries: bfloat16 [32, 128, 576], P('expert', 'head'), may hold values from -136 to 136
- kv_cache: bfloat16 [32, 12288, 576], P('expert', 'head'), may hold values from -4 to 4
- block_ids: int32 [32, 32], P('expert'), may hold values from 0 to 191, as said below
- w_uv: bfloat16 [128, 512, 128], P('head'), may hold values from -0.25 to 0.25
- o_proj: bfloat16 [16384, 3584], P('head', 'expert'), may hold values from -0.046875 to 0.046875
- residual: bfloat16 [32, 3584], P(None, 'expert'), may hold values from -6 to 6
- moe_gain: bfloat16 [3584], P('expert'), may hold values from 0.099609375 to 1.8984375
- w_gate: bfloat16 [32, 3584, 2048], P('expert', None, 'head'), may hold values from -0.09375 to 0.09375
- w_up: bfloat16 [32, 3584, 2048], P('expert', None, 'head'), may hold values from -0.09375 to 0.09375
- w_down: bfloat16 [32, 2048, 3584], P('expert', 'head'), may hold values from -0.125 to 0.125
- expert_ids: int32 [32, 8], replicated, may hold values from 0 to 31, all different within a row; in each aligned block of 32 rows (0 to 31, 32 to 63, ...) at most 16 rows name the same one
- gate_weights: float32 [32, 8], replicated, may hold values from 0.05 to 0.3
Outputs:
- layer_output: bfloat16 [32, 3584], P('head', 'expert')
The draws below stay inside these ranges and needn't reach their ends.
Inputs may be any that keep to these rules, and one draw needn't show every extreme that they name: `block_ids`: each row names 32 different blocks. `expert_ids`: each row names 8 different experts; no expert is named by more than 16 of the 32 rows, a bound that some block reaches.
All inputs are finite; a program needn't handle non-finite values.
Results may differ from the reference program's by a relative error of at most 0.0075.
Values may be sent and summed in bfloat16 or wider, within the bound.
No kernel may reach another device: no remote copies, remote signals or barrier semaphores. Data moves between devices by JAX's collectives and lax.ppermute only.
A program may use at most 64 MiB of HBM per device.

```python
import math
import jax
import jax.numpy as jnp
import numpy as np
from jax import lax

D = 3584
H = 128
LAT = 512
VD = 128
FF = 2048
TOP = 8
BLK = 64
SEL = 32
NBLK = 192
ROWS = 32
EXPERTS = 32
CAP = 16
CTX = 12288
QK = 576


def pick_blocks(key):
    row_keys = jax.random.split(jax.random.fold_in(key, 11), ROWS)
    return jax.vmap(lambda row_key: jax.random.permutation(row_key, NBLK)[:SEL])(row_keys).astype(jnp.int32)


def drawn_normal(key, array_shape, clip_at):
    return jnp.clip(jax.random.normal(key, array_shape, jnp.float32), -clip_at, clip_at)


def draw_block_ids(key, part):
    return pick_blocks(key)


def draw_kv_cache(key, part):
    cache_key = jax.random.fold_in(key, 12)
    cache_vals = drawn_normal(cache_key, (ROWS, CTX, QK), 4.0)
    return cache_vals.astype(jnp.bfloat16)


def draw_queries(key, part):
    query_key = jax.random.fold_in(key, 3)
    query_vals = drawn_normal(query_key, (ROWS, H, QK), 4.0)
    return query_vals.astype(jnp.bfloat16)


def level_of(own_key, extent, shards, smallest, largest):
    def one(axis_at, shards_of):
        heights = jax.random.uniform(jax.random.fold_in(jax.random.fold_in(own_key, 6), axis_at), (shards_of,), jnp.float32, smallest / len(shards), largest / len(shards))
        return jnp.repeat(jnp.exp(heights), extent[axis_at] // shards_of).reshape((-1,) + (1,) * (len(extent) - axis_at - 1))

    loudness = one(*shards[0])
    for cut in shards[1:]:
        loudness = loudness * one(*cut)
    return loudness


def deal_out(own_key, own, number, rows, count, top, limit, lean):
    ranking = jax.random.permutation(own_key, count)
    crowded, common = load_shares(count, rows * top, limit, lean, True), load_shares(count, rows * top, limit, lean, False)
    places = jnp.arange(count)

    def named(tallies, rotation):
        used = int((tallies > 0).sum())
        fixed = max(1, used // 4)
        shifted = fixed + (places - fixed + rotation * (used - fixed)) % max(1, count - fixed)
        return jnp.zeros((count,), jnp.int32).at[ranking[jnp.where(places < fixed, places, shifted)]].set(jnp.asarray(tallies, jnp.int32))

    tallies = jnp.where(number % 4 == 0, named(crowded, number // 4), named(common, number - number // 4 - 1))
    mixed = jax.random.permutation(jax.random.fold_in(own, 3), count)
    source_of, receiver = mixed[0:count // 2 * 2:2], mixed[1:count // 2 * 2:2]
    slack = jnp.minimum(tallies[source_of] - 1, limit - tallies[receiver]) // 2
    slack = jnp.where((source_of == ranking[0]) | (receiver == ranking[0]) | (tallies[receiver] == 0), 0, jnp.maximum(slack, 0))
    shifted = jax.random.randint(jax.random.fold_in(own, 4), (count // 2,), 0, 1 << 20) % (slack + 1)
    tallies = tallies.at[source_of].add(-shifted).at[receiver].add(shifted)
    members = jnp.searchsorted(jnp.cumsum(tallies), jnp.arange(rows * top), side="right").astype(jnp.int32)
    listing = members.reshape(top, rows).T
    listing = listing[jax.random.permutation(jax.random.fold_in(own, 1), rows)]
    rotation = jax.random.randint(jax.random.fold_in(own, 2), (rows, 1), 0, top)
    return jnp.take_along_axis(listing, (jnp.arange(top)[None, :] + rotation) % top, axis=1)


def load_shares(count, total, most, skew, full):
    weights = [(1 << 20) // math.isqrt(standing ** skew) + 1 for standing in range(1, count + 1)]
    largest = most if full else min(most, max(-(-total // count), total * weights[0] // sum(weights)))
    least = 1 if total - largest >= count - 1 else 0
    holding, spare = [largest] + [least] * (count - 1), total - largest - least * (count - 1)
    while spare > 0:
        movable = [i for i in range(1, count) if holding[i] < largest] or [i for i in range(1, count) if holding[i] < most]
        mass, budget = sum([weights[i] for i in movable]), spare
        for i in movable:
            extra = min(most - holding[i], max(1, budget * weights[i] // mass), spare)
            holding[i] = holding[i] + extra
            spare = spare - extra
    return np.array(holding)


def scatter_about(stream_key, dims, spread, bound, shards=(), kind=jnp.bfloat16):
    values = spread * jax.random.normal(stream_key, dims, jnp.float32)
    if shards:
        values = values * level_of(stream_key, dims, shards, -0.22, 0.18)
    return jnp.clip(values, -bound, bound).astype(kind)


def setup_inputs(seed: int = 0) -> dict:
    arg_keys = jax.random.split(jax.random.key(seed), 13)
    queries = draw_queries(jax.random.fold_in(arg_keys[12], 71), 0)
    kv_cache = draw_kv_cache(jax.random.fold_in(arg_keys[12], 71), 0)
    block_ids = draw_block_ids(jax.random.fold_in(arg_keys[12], 71), 0)
    w_uv = scatter_about(arg_keys[3], (H, LAT, VD), LAT ** -0.5, 0.25, ((0, 16),))
    o_proj = scatter_about(arg_keys[4], (H * VD, D), (H * VD) ** -0.5, 0.046875, ((0, 16), (1, 32)))
    residual = scatter_about(arg_keys[5], (ROWS, D), 1.0, 6.0, ((1, 32),))
    moe_gain = jnp.clip(1.0 + 0.18 * jax.random.normal(arg_keys[6], (D,), jnp.float32), 0.099609375, 1.8984375).astype(jnp.bfloat16)
    w_gate = scatter_about(arg_keys[7], (EXPERTS, D, FF), D ** -0.5, 0.09375, ((0, 32), (2, 16)))
    w_up = scatter_about(arg_keys[8], (EXPERTS, D, FF), D ** -0.5, 0.09375, ((0, 32), (2, 16)))
    w_down = scatter_about(arg_keys[9], (EXPERTS, FF, D), FF ** -0.5, 0.125, ((0, 32), (1, 16)))
    expert_ids_keys = jax.random.split(jax.random.fold_in(arg_keys[10], 1), ROWS // ROWS)
    expert_ids_turns = jax.random.permutation(jax.random.fold_in(arg_keys[10], 3), ROWS // ROWS)
    expert_ids = jax.vmap(lambda own, number: deal_out(jax.random.fold_in(arg_keys[10], 2), own, number, ROWS, EXPERTS, TOP, CAP, 2))(expert_ids_keys, expert_ids_turns).reshape((ROWS, TOP))
    gate_weights = jnp.clip(jax.random.uniform(arg_keys[11], (ROWS, TOP), jnp.float32, 0.05, 0.3), 0.05, 0.3)
    return {"queries": queries, "kv_cache": kv_cache, "block_ids": block_ids, "w_uv": w_uv, "o_proj": o_proj, "residual": residual, "moe_gain": moe_gain, "w_gate": w_gate, "w_up": w_up, "w_down": w_down, "expert_ids": expert_ids, "gate_weights": gate_weights}


score_scale = 192 ** (-0.5)
norm_eps = 1e-06

def slot_tables(expert_ids, gate_weights, experts, capacity):
    onehot = expert_ids[:, :, None] == jnp.arange(experts, dtype=jnp.int32)[None, None, :]
    picked = lax.optimization_barrier(jnp.sum(onehot.astype(jnp.int32), axis=1))
    weight = lax.optimization_barrier(jnp.sum(jnp.where(onehot, gate_weights[:, :, None], jnp.zeros_like(gate_weights[:, :, None])), axis=1))
    before = jnp.cumsum(picked, axis=0) - picked
    matched = (picked[:, :, None] == 1) & (before[:, :, None] == jnp.arange(capacity, dtype=jnp.int32)[None, None, :])
    dispatch_map = matched.astype(gate_weights.dtype)
    combine_map = dispatch_map * weight[:, :, None]
    row_count = expert_ids.shape[0]
    return (dispatch_map.reshape(row_count, experts * capacity), combine_map.reshape(row_count, experts * capacity))

def reference(queries, kv_cache, block_ids, w_uv, o_proj, residual, moe_gain, w_gate, w_up, w_down, expert_ids, gate_weights):
    offsets = jnp.arange(BLK, dtype=jnp.int32)
    wide_uv = w_uv.astype(jnp.float32)

    def one_row(bundle):
        one_query, one_cache, one_picks = bundle
        token_pos = (one_picks.astype(jnp.int32)[:, None] * BLK + offsets[None, :]).reshape(-1)
        chosen = jnp.take(one_cache, token_pos, axis=0)
        scores = jnp.dot(one_query, chosen.T, preferred_element_type=jnp.float32) * score_scale
        highest = lax.optimization_barrier(jnp.max(scores, axis=1, keepdims=True))
        exponent = jnp.exp(scores - highest)
        denominator = lax.optimization_barrier(jnp.sum(exponent, axis=1, keepdims=True))
        latent = jnp.dot(exponent.astype(jnp.bfloat16), chosen[:, :LAT], preferred_element_type=jnp.float32)
        attended = (latent / denominator).astype(jnp.bfloat16)
        head_vals = jnp.einsum('hc,hcv->hv', attended.astype(jnp.float32), wide_uv)
        return head_vals.astype(jnp.bfloat16).reshape(-1)
    head_flat = lax.map(one_row, (queries, kv_cache, block_ids))
    attn = jnp.dot(head_flat, o_proj, preferred_element_type=jnp.float32)
    mixed_state = (residual.astype(jnp.float32) + attn).astype(jnp.bfloat16)
    widened = mixed_state.astype(jnp.float32)
    mean_square = lax.optimization_barrier(jnp.mean(widened * widened, axis=1, keepdims=True))
    normed = (widened * lax.rsqrt(mean_square + norm_eps) * moe_gain.astype(jnp.float32)[None, :]).astype(jnp.bfloat16)
    dispatch_map, combine_map = slot_tables(expert_ids, gate_weights, EXPERTS, CAP)
    slot_rows = jnp.dot(dispatch_map.T.astype(jnp.bfloat16), normed, preferred_element_type=jnp.float32)
    slot_rows = slot_rows.astype(jnp.bfloat16).reshape(EXPERTS, CAP, D)

    def one_expert(bundle):
        tokens, gate_mat, up_mat, down_mat = bundle
        gate_act = jnp.dot(tokens, gate_mat, preferred_element_type=jnp.float32)
        up_act = jnp.dot(tokens, up_mat, preferred_element_type=jnp.float32)
        hidden = (jax.nn.silu(gate_act) * up_act).astype(jnp.bfloat16)
        return jnp.dot(hidden, down_mat, preferred_element_type=jnp.float32)
    outputs = lax.map(one_expert, (slot_rows, w_gate, w_up, w_down))
    moe_out = jnp.dot(combine_map, outputs.reshape(EXPERTS * CAP, D), precision=lax.Precision.HIGHEST, preferred_element_type=jnp.float32)
    return (mixed_state.astype(jnp.float32) + moe_out).astype(jnp.bfloat16)
```

```python
import functools

import jax
import jax.numpy as jnp
from jax import lax
from jax.experimental import pallas as pl
from jax.experimental.pallas import tpu as pltpu
from jax.sharding import PartitionSpec as P

LAT = 512
BLK = 64
LANES = 128
NEG = -1e30

score_scale = 192 ** (-0.5)
norm_eps = 1e-06

f32 = jnp.float32
bf16 = jnp.bfloat16


def call(body, out_shape, in_specs, *operands, scratch=()):
    return pl.pallas_call(
        body,
        out_shape=out_shape,
        in_specs=in_specs,
        out_specs=pl.BlockSpec(memory_space=pltpu.VMEM),
        scratch_shapes=scratch,
        compiler_params=pltpu.CompilerParams(vmem_limit_bytes=48 * 1024 * 1024),
    )(*operands)


VM = pl.BlockSpec(memory_space=pltpu.VMEM)
SM = pl.BlockSpec(memory_space=pltpu.SMEM)


def exchange(blocks, axis):
    return lax.all_to_all(blocks, axis, split_axis=0, concat_axis=0, tiled=True)


def attend_body(picks_ref, q_ref, kv_ref, out_ref):
    tokens = kv_ref.shape[0]
    first_block = lax.axis_index("head") * (tokens // BLK)
    block_of = lax.broadcasted_iota(jnp.int32, (8, tokens), 1) // BLK + first_block
    chosen = block_of == picks_ref[0, 0]
    for i in range(1, picks_ref.shape[1]):
        chosen = chosen | (block_of == picks_ref[0, i])
    chosen = chosen[0:1]
    scores = (
        lax.dot_general(q_ref[...], kv_ref[...], (((1,), (1,)), ((), ())), preferred_element_type=f32)
        * score_scale
    )
    scores = jnp.where(chosen, scores, NEG)
    highest = jnp.max(scores, axis=1, keepdims=True)
    top = highest.astype(bf16).astype(f32)
    rest = (highest - top).astype(bf16).astype(f32)
    weights = jnp.where(chosen, jnp.exp(scores - (top + rest)), 0.0)
    total = jnp.sum(weights, axis=1, keepdims=True)
    latent = jnp.dot(weights.astype(bf16), kv_ref[:, :LAT], preferred_element_type=f32)
    total_top = total.astype(bf16).astype(f32)
    total_rest = total - total_top
    lane = lax.broadcasted_iota(jnp.int32, (q_ref.shape[0], LANES), 1)
    stats = jnp.where(
        lane == 0, top, jnp.where(lane == 1, rest, jnp.where(lane == 2, total_top, total_rest))
    )
    out_ref[:, :LAT] = latent.astype(bf16)
    out_ref[:, LAT:] = stats.astype(bf16)


def values_body(parts_ref, uv_ref, gain_ref, out_ref):
    parts = parts_ref[...].astype(f32)
    heads = parts.shape[1]
    stats = parts[:, :, LAT:]
    scale = stats[:, :, 0:1] + stats[:, :, 1:2]
    total = stats[:, :, 2:3] + stats[:, :, 3:4]
    factor = jnp.exp(scale - jnp.max(scale, axis=0, keepdims=True))
    denominator = jnp.sum(factor * total, axis=0)
    attended = jnp.sum(factor * parts[:, :, :LAT], axis=0) / denominator
    row = lax.broadcasted_iota(jnp.int32, attended.shape, 0)
    spread = jnp.concatenate(
        [jnp.where(row == j, attended, 0.0).astype(bf16) for j in range(heads)], axis=1
    )
    head_vals = jnp.dot(spread, uv_ref[...], preferred_element_type=f32)
    gain = gain_ref[...].astype(f32)
    gain = jnp.concatenate([gain, jnp.zeros((1, LANES - gain.shape[1]), f32)], axis=1)
    both = jnp.concatenate([head_vals, jnp.broadcast_to(gain, (8, LANES))], axis=0).astype(bf16)
    out_ref[...] = jnp.broadcast_to(both[None], out_ref.shape)


def project_body(vals_ref, o_ref, out_ref):
    vals = vals_ref[...].astype(f32)
    wide = jnp.concatenate([vals[:, j, :] for j in range(8)], axis=1).astype(bf16)
    part = jnp.dot(wide, o_ref[...], preferred_element_type=f32).astype(bf16)
    part = jnp.concatenate(
        [part, jnp.zeros((part.shape[0], LANES - part.shape[1]), bf16)], axis=1
    )
    out_ref[...] = jnp.broadcast_to(part[None], out_ref.shape)


def mix_body(parts_ref, residual_ref, out_ref):
    attn = jnp.sum(parts_ref[...].astype(f32), axis=0)
    residual = residual_ref[...].astype(f32)
    residual = jnp.concatenate(
        [residual, jnp.zeros((residual.shape[0], LANES - residual.shape[1]), f32)], axis=1
    )
    mixed = (residual + attn).astype(bf16)
    out_ref[...] = jnp.broadcast_to(mixed[None], out_ref.shape)


def expert_body(mixed_ref, vals_ref, gate_ref, up_ref, down_ref, ids_ref, gw_ref, out_ref):
    owners, rows = mixed_ref.shape[:2]
    width = gate_ref.shape[0] // owners
    features = gate_ref.shape[0]
    mixed = mixed_ref[...].astype(f32)
    lane = lax.broadcasted_iota(jnp.int32, (1, 1, LANES), 2)
    mixed = jnp.where(lane < width, mixed, 0.0)
    squares = jnp.sum(jnp.sum(mixed * mixed, axis=0), axis=1, keepdims=True)
    scale = lax.rsqrt(squares / features + norm_eps)
    gain = vals_ref[:, 8:16, :].astype(f32)[:, 0:1, :]
    gain = jnp.where(lane < width, gain, 0.0)
    normed = (mixed * scale[None] * gain).astype(bf16)
    gate_act = jnp.zeros((rows, gate_ref.shape[1]), f32)
    up_act = jnp.zeros((rows, up_ref.shape[1]), f32)
    for i in range(owners):
        mine = normed[i][:, :width]
        gate_act += jnp.dot(mine, gate_ref[i * width : (i + 1) * width, :], preferred_element_type=f32)
        up_act += jnp.dot(mine, up_ref[i * width : (i + 1) * width, :], preferred_element_type=f32)
    hidden = (gate_act / (1.0 + jnp.exp(-gate_act)) * up_act).astype(bf16)
    here = lax.axis_index("expert")
    weight = jnp.sum(jnp.where(ids_ref[...] == here, gw_ref[...], 0.0), axis=1, keepdims=True)
    outcome = jnp.dot(hidden, down_ref[...], preferred_element_type=f32) * weight
    pad = jnp.zeros((rows, LANES - width), f32)
    for i in range(owners):
        out_ref[i] = jnp.concatenate(
            [outcome[:, i * width : (i + 1) * width], pad], axis=1
        ).astype(bf16)


def gather_body(parts_ref, mixed_ref, out_ref):
    share = jnp.sum(parts_ref[...].astype(f32), axis=0)
    first = lax.axis_index("head") == 0
    share = share + jnp.where(first, mixed_ref[0].astype(f32), 0.0)
    groups, rows = out_ref.shape[0], share.shape[0]
    for i in range(groups):
        group = i * rows // groups // 8
        out_ref[i] = share[group * 8 : group * 8 + 8]


def local(
    queries,
    kv_cache,
    block_ids,
    w_uv,
    o_proj,
    residual,
    moe_gain,
    w_gate,
    w_up,
    w_down,
    expert_ids,
    gate_weights,
):
    head_n = lax.axis_size("head")
    expert_n = lax.axis_size("expert")
    heads, width = queries.shape[1:]
    rows = expert_ids.shape[0]
    columns = o_proj.shape[1]
    row_share = rows // head_n

    asked = exchange(jnp.broadcast_to(queries, (head_n, heads, width)), "head")
    shares = call(
        attend_body,
        jax.ShapeDtypeStruct((head_n * heads, LAT + LANES), bf16),
        [SM, VM, VM],
        block_ids,
        asked.reshape(head_n * heads, width),
        kv_cache[0],
    )
    shares = exchange(shares.reshape(head_n, heads, LAT + LANES), "head")
    vals = call(
        values_body,
        jax.ShapeDtypeStruct((expert_n, 16, LANES), bf16),
        [VM, VM, VM],
        shares,
        w_uv.reshape(heads * LAT, -1),
        moe_gain[None, :],
    )
    vals = exchange(vals, "expert")
    attn = call(
        project_body,
        jax.ShapeDtypeStruct((head_n, rows, LANES), bf16),
        [VM, VM],
        vals,
        o_proj,
    )
    attn = exchange(attn, "head")
    mixed = call(
        mix_body,
        jax.ShapeDtypeStruct((expert_n, rows, LANES), bf16),
        [VM, VM],
        attn,
        residual,
    )
    features = exchange(mixed, "expert")
    outcome = call(
        expert_body,
        jax.ShapeDtypeStruct((expert_n, rows, LANES), bf16),
        [VM] * 7,
        features,
        vals,
        w_gate[0],
        w_up[0],
        w_down[0],
        expert_ids,
        gate_weights,
    )
    outcome = exchange(outcome, "expert")
    moe = call(
        gather_body,
        jax.ShapeDtypeStruct((head_n, 8, LANES), f32),
        [VM, VM],
        outcome,
        mixed,
    )
    moe = jnp.sum(exchange(moe, "head"), axis=0)
    first = lax.axis_index("head") * row_share % 8
    return lax.dynamic_slice(moe, (first, 0), (row_share, columns)).astype(bf16)


def solution(mesh):
    in_specs = (
        P("expert", "head", None),
        P("expert", "head", None),
        P("expert", None),
        P("head", None, None),
        P("head", "expert"),
        P(None, "expert"),
        P("expert"),
        P("expert", None, "head"),
        P("expert", None, "head"),
        P("expert", "head", None),
        P(),
        P(),
    )
    out_specs = P("head", "expert")
    return jax.shard_map(local, mesh=mesh, in_specs=in_specs, out_specs=out_specs, check_vma=False)
```

```python
import functools

import jax
import jax.numpy as jnp
from jax import lax
from jax.experimental import pallas as pl
from jax.experimental.pallas import tpu as pltpu
from jax.sharding import PartitionSpec as P

LAT = 512
BLK = 64
LANES = 128
NEG = -1e30

score_scale = 192 ** (-0.5)
norm_eps = 1e-06

f32 = jnp.float32
bf16 = jnp.bfloat16


VM = pl.BlockSpec(memory_space=pltpu.VMEM)
SM = pl.BlockSpec(memory_space=pltpu.SMEM)
shape = jax.ShapeDtypeStruct


def call(body, out_shape, in_specs, *operands):
    return pl.pallas_call(
        body,
        out_shape=out_shape,
        in_specs=in_specs,
        out_specs=jax.tree.map(lambda _: VM, out_shape),
        compiler_params=pltpu.CompilerParams(vmem_limit_bytes=48 * 1024 * 1024),
    )(*operands)


def exchange(blocks, axis):
    return lax.all_to_all(blocks, axis, split_axis=0, concat_axis=0, tiled=True)


def attend_body(picks_ref, q_ref, kv_ref, out_ref):
    tokens = kv_ref.shape[0]
    first_block = lax.axis_index("head") * (tokens // BLK)
    block_of = lax.broadcasted_iota(jnp.int32, (8, tokens), 1) // BLK + first_block
    chosen = block_of == picks_ref[0, 0]
    for i in range(1, picks_ref.shape[1]):
        chosen = chosen | (block_of == picks_ref[0, i])
    chosen = chosen[0:1]
    scores = (
        lax.dot_general(q_ref[...], kv_ref[...], (((1,), (1,)), ((), ())), preferred_element_type=f32)
        * score_scale
    )
    scores = jnp.where(chosen, scores, NEG)
    highest = jnp.max(scores, axis=1, keepdims=True)
    top = highest.astype(bf16).astype(f32)
    rest = (highest - top).astype(bf16).astype(f32)
    weights = jnp.where(chosen, jnp.exp(scores - (top + rest)), 0.0)
    total = jnp.sum(weights, axis=1, keepdims=True)
    latent = jnp.dot(weights.astype(bf16), kv_ref[:, :LAT], preferred_element_type=f32)
    total_top = total.astype(bf16).astype(f32)
    total_rest = total - total_top
    lane = lax.broadcasted_iota(jnp.int32, (q_ref.shape[0], LANES), 1)
    stats = jnp.where(
        lane == 0, top, jnp.where(lane == 1, rest, jnp.where(lane == 2, total_top, total_rest))
    )
    out_ref[:, :LAT] = latent.astype(bf16)
    out_ref[:, LAT:] = stats.astype(bf16)


def copies_body(one_ref, out_ref):
    out_ref[...] = jnp.broadcast_to(one_ref[...], out_ref.shape)


def tables_body(
    ids_ref, gw_ref, residual_ref, gain_ref, dispatch_ref, combine_ref, weight_ref, residual_out, gain_out
):
    rows, top = ids_ref.shape
    slots = combine_ref.shape[1]
    capacity = weight_ref.shape[0]
    ids = ids_ref[...]
    expert = lax.broadcasted_iota(jnp.int32, (rows, LANES), 1)
    picked = jnp.zeros((rows, LANES), f32)
    for k in range(top):
        picked = picked + (ids[:, k : k + 1] == expert).astype(f32)
    earlier = lax.broadcasted_iota(jnp.int32, (rows, rows), 1) < lax.broadcasted_iota(
        jnp.int32, (rows, rows), 0
    )
    before = jnp.dot(
        earlier.astype(bf16), picked.astype(bf16), preferred_element_type=f32
    )
    held = jnp.where(picked > 0.5, before, -1.0).astype(bf16)
    spread = lax.broadcasted_iota(jnp.int32, (LANES, slots), 0) == (
        lax.broadcasted_iota(jnp.int32, (LANES, slots), 1) // capacity
    )
    along = jnp.dot(held, spread.astype(bf16), preferred_element_type=f32)
    slot = lax.broadcasted_iota(jnp.int32, (rows, slots), 1) % capacity
    combine_ref[...] = (along == slot.astype(f32)).astype(bf16)
    spread = lax.broadcasted_iota(jnp.int32, (slots, LANES), 1) == (
        lax.broadcasted_iota(jnp.int32, (slots, LANES), 0) // capacity
    )
    down = lax.dot_general(
        spread.astype(bf16), held, (((1,), (1,)), ((), ())), preferred_element_type=f32
    )
    slot = lax.broadcasted_iota(jnp.int32, (slots, rows), 0) % capacity
    dispatch_ref[...] = (down == slot.astype(f32)).astype(bf16)
    here = lax.axis_index("expert")
    weight = jnp.sum(jnp.where(ids == here, gw_ref[...], 0.0), axis=1, keepdims=True)
    mine = jnp.sum(
        jnp.where(expert == here, held.astype(f32), 0.0), axis=1, keepdims=True
    )
    by_slot = jnp.sum(jnp.where(mine == expert.astype(f32), weight, 0.0), axis=0, keepdims=True)
    by_slot = jnp.broadcast_to(by_slot, (capacity, LANES))
    diagonal = lax.broadcasted_iota(jnp.int32, (capacity, LANES), 1) == lax.broadcasted_iota(
        jnp.int32, (capacity, LANES), 0
    )
    by_slot = jnp.sum(jnp.where(diagonal, by_slot, 0.0), axis=1, keepdims=True)
    weight_ref[...] = jnp.broadcast_to(by_slot, weight_ref.shape)
    width = residual_ref.shape[1]
    residual_out[...] = jnp.concatenate(
        [residual_ref[...].astype(f32), jnp.zeros((rows, LANES - width), f32)], axis=1
    )
    gain = jnp.concatenate(
        [gain_ref[...].astype(f32), jnp.zeros((1, LANES - width), f32)], axis=1
    )
    gain_out[...] = jnp.broadcast_to(gain, gain_out.shape)


def values_body(parts_ref, uv_ref, out_ref):
    parts = parts_ref[...].astype(f32)
    heads = parts.shape[1]
    stats = parts[:, :, LAT:]
    scale = stats[:, :, 0:1] + stats[:, :, 1:2]
    total = stats[:, :, 2:3] + stats[:, :, 3:4]
    factor = jnp.exp(scale - jnp.max(scale, axis=0, keepdims=True))
    denominator = jnp.sum(factor * total, axis=0)
    attended = jnp.sum(factor * parts[:, :, :LAT], axis=0) / denominator
    row = lax.broadcasted_iota(jnp.int32, attended.shape, 0)
    spread = jnp.concatenate(
        [jnp.where(row == j, attended, 0.0).astype(bf16) for j in range(heads)], axis=1
    )
    head_vals = jnp.dot(spread, uv_ref[...], preferred_element_type=f32).astype(bf16)
    out_ref[...] = jnp.broadcast_to(head_vals[None], out_ref.shape)


def project_body(vals_ref, o_ref, out_ref):
    vals = vals_ref[...].astype(f32)
    wide = jnp.concatenate([vals[:, j, :] for j in range(vals.shape[1])], axis=1).astype(bf16)
    part = jnp.dot(wide, o_ref[...], preferred_element_type=f32).astype(bf16)
    part = jnp.concatenate(
        [part, jnp.zeros((part.shape[0], LANES - part.shape[1]), bf16)], axis=1
    )
    out_ref[...] = jnp.broadcast_to(part[None], out_ref.shape)


def mix_body(width, parts_ref, residual_ref, gain_ref, dispatch_ref, out_ref, mixed_ref):
    attn = jnp.sum(parts_ref[...].astype(f32), axis=0)
    mixed = (residual_ref[...] + attn).astype(bf16).astype(f32)
    mixed_ref[...] = mixed
    squares = jnp.sum(mixed * mixed, axis=1, keepdims=True)
    top = squares.astype(bf16).astype(f32)
    lane = lax.broadcasted_iota(jnp.int32, mixed.shape, 1)
    scaled = jnp.where(
        lane == width, top, jnp.where(lane == width + 1, squares - top, mixed * gain_ref[0:1])
    )
    slots = jnp.dot(dispatch_ref[...], scaled.astype(bf16), preferred_element_type=f32)
    out_ref[...] = slots.astype(bf16).reshape(out_ref.shape)


def expert_body(slots_ref, gate_ref, up_ref, down_ref, weight_ref, out_ref):
    owners, capacity = slots_ref.shape[:2]
    features, units = gate_ref.shape
    width = features // owners
    lane = lax.broadcasted_iota(jnp.int32, (capacity, LANES), 1)
    stats = jnp.sum(slots_ref[...].astype(f32), axis=0)
    stats = jnp.where((lane == width) | (lane == width + 1), stats, 0.0)
    scale = lax.rsqrt(jnp.sum(stats, axis=1, keepdims=True) / features + norm_eps)
    both = jnp.zeros((capacity, 2 * units), f32)
    for i in range(owners):
        part = slice(i * width, (i + 1) * width)
        weights = jnp.concatenate([gate_ref[part, :], up_ref[part, :]], axis=1)
        both += jnp.dot(slots_ref[i][:, :width], weights, preferred_element_type=f32)
    both = both * scale
    gate_act, up_act = both[:, :units], both[:, units:]
    hidden = (gate_act / (1.0 + jnp.exp(-gate_act)) * up_act).astype(bf16)
    outcome = jnp.dot(hidden, down_ref[...], preferred_element_type=f32) * weight_ref[:, 0:1]
    pad = jnp.zeros((capacity, LANES - width), f32)
    for i in range(owners):
        out_ref[i] = jnp.concatenate(
            [outcome[:, i * width : (i + 1) * width], pad], axis=1
        ).astype(bf16)


def gather_body(parts_ref, combine_ref, mixed_ref, out_ref):
    parts = parts_ref[...].reshape(combine_ref.shape[1], LANES)
    share = jnp.dot(combine_ref[...], parts, preferred_element_type=f32)
    share = share + jnp.where(lax.axis_index("head") == 0, mixed_ref[...], 0.0)
    groups, rows = out_ref.shape[0], share.shape[0]
    for i in range(groups):
        group = i * rows // groups // 8
        out_ref[i] = share[group * 8 : group * 8 + 8]


def local(
    queries,
    kv_cache,
    block_ids,
    w_uv,
    o_proj,
    residual,
    moe_gain,
    w_gate,
    w_up,
    w_down,
    expert_ids,
    gate_weights,
):
    head_n = lax.axis_size("head")
    expert_n = lax.axis_size("expert")
    heads, width = queries.shape[1:]
    rows, top = expert_ids.shape
    columns = o_proj.shape[1]
    row_share = rows // head_n
    capacity = min(2 * (rows // expert_n) * top, rows)
    slots = expert_n * capacity

    asked = call(copies_body, shape((head_n, heads, width), bf16), [VM], queries)
    asked = exchange(asked, "head")
    dispatch, combine, weight, residual_wide, gain = call(
        tables_body,
        (
            shape((slots, rows), bf16),
            shape((rows, slots), bf16),
            shape((capacity, LANES), f32),
            shape((rows, LANES), f32),
            shape((8, LANES), f32),
        ),
        [VM] * 4,
        expert_ids,
        gate_weights,
        residual,
        moe_gain[None, :],
    )
    shares = call(
        attend_body,
        shape((head_n * heads, LAT + LANES), bf16),
        [SM, VM, VM],
        block_ids,
        asked.reshape(head_n * heads, width),
        kv_cache[0],
    )
    shares = exchange(shares.reshape(head_n, heads, LAT + LANES), "head")
    vals = call(
        values_body,
        shape((expert_n, heads, w_uv.shape[2]), bf16),
        [VM, VM],
        shares,
        w_uv.reshape(heads * LAT, -1),
    )
    vals = exchange(vals, "expert")
    attn = call(project_body, shape((head_n, rows, LANES), bf16), [VM, VM], vals, o_proj)
    attn = exchange(attn, "head")
    tokens, mixed = call(
        functools.partial(mix_body, columns),
        (shape((expert_n, capacity, LANES), bf16), shape((rows, LANES), f32)),
        [VM] * 4,
        attn,
        residual_wide,
        gain,
        dispatch,
    )
    tokens = exchange(tokens, "expert")
    outcome = call(
        expert_body,
        shape((expert_n, capacity, LANES), bf16),
        [VM] * 5,
        tokens,
        w_gate[0],
        w_up[0],
        w_down[0],
        weight,
    )
    outcome = exchange(outcome, "expert")
    moe = call(gather_body, shape((head_n, 8, LANES), f32), [VM] * 3, outcome, combine, mixed)
    moe = jnp.sum(exchange(moe, "head"), axis=0)
    first = lax.axis_index("head") * row_share % 8
    return lax.dynamic_slice(moe, (first, 0), (row_share, columns)).astype(bf16)


def solution(mesh):
    in_specs = (
        P("expert", "head", None),
        P("expert", "head", None),
        P("expert", None),
        P("head", None, None),
        P("head", "expert"),
        P(None, "expert"),
        P("expert"),
        P("expert", None, "head"),
        P("expert", None, "head"),
        P("expert", "head", None),
        P(),
        P(),
    )
    out_specs = P("head", "expert")
    return jax.shard_map(local, mesh=mesh, in_specs=in_specs, out_specs=out_specs, check_vma=False)
```

```python
import functools

import jax
import jax.numpy as jnp
from jax import lax
from jax.experimental import pallas as pl
from jax.experimental.pallas import tpu as pltpu
from jax.sharding import PartitionSpec as P

LAT = 512
BLK = 64
LANES = 128
NEG = -1e30

score_scale = 192 ** (-0.5)
norm_eps = 1e-06

f32 = jnp.float32
bf16 = jnp.bfloat16


VM = pl.BlockSpec(memory_space=pltpu.VMEM)
SM = pl.BlockSpec(memory_space=pltpu.SMEM)
shape = jax.ShapeDtypeStruct


def call(body, out_shape, in_specs, *operands):
    return pl.pallas_call(
        body,
        out_shape=out_shape,
        in_specs=in_specs,
        out_specs=jax.tree.map(lambda _: VM, out_shape),
        compiler_params=pltpu.CompilerParams(vmem_limit_bytes=48 * 1024 * 1024),
    )(*operands)


def exchange(blocks, axis):
    return lax.all_to_all(blocks, axis, split_axis=0, concat_axis=0, tiled=True)


def attend_body(chosen_ref, q_ref, kv_ref, out_ref):
    chosen = chosen_ref[0:1] > 0.5
    scores = (
        jnp.dot(q_ref[...], kv_ref[...], preferred_element_type=f32) * score_scale
    )
    scores = jnp.where(chosen, scores, NEG)
    highest = jnp.max(scores, axis=1, keepdims=True)
    top = highest.astype(bf16).astype(f32)
    rest = (highest - top).astype(bf16).astype(f32)
    weights = jnp.where(chosen, jnp.exp(scores - (top + rest)), 0.0)
    total = jnp.sum(weights, axis=1, keepdims=True)
    latent = lax.dot_general(
        weights.astype(bf16), kv_ref[:LAT, :], (((1,), (1,)), ((), ())), preferred_element_type=f32
    )
    total_top = total.astype(bf16).astype(f32)
    total_rest = total - total_top
    lane = lax.broadcasted_iota(jnp.int32, (q_ref.shape[0], LANES), 1)
    stats = jnp.where(
        lane == 0, top, jnp.where(lane == 1, rest, jnp.where(lane == 2, total_top, total_rest))
    )
    out_ref[:, :LAT] = latent.astype(bf16)
    out_ref[:, LAT:] = stats.astype(bf16)


def copies_body(one_ref, out_ref):
    out_ref[...] = jnp.broadcast_to(one_ref[...], out_ref.shape)


def stage_body(
    ids_any, gw_any, residual_any, gain_any, picks_any, o_any, cache_any,
    dispatch_ref, combine_ref, weight_ref, residual_out, gain_out, chosen_ref, o_out, cache_out,
    ids_ref, gw_ref, residual_ref, gain_ref, picks_ref, o_ref, sems,
):
    pairs = (
        (ids_any, ids_ref),
        (gw_any, gw_ref),
        (residual_any, residual_ref),
        (gain_any, gain_ref),
        (picks_any, picks_ref),
        (o_any, o_ref),
        (cache_any, cache_out),
    )
    copies = [pltpu.make_async_copy(a, b, sems.at[i]) for i, (a, b) in enumerate(pairs)]
    for copy in copies:
        copy.start()
    for copy in copies:
        copy.wait()
    o_out[...] = o_ref[...].T
    tokens = chosen_ref.shape[1]
    first_block = lax.axis_index("head") * (tokens // BLK)
    block_of = lax.broadcasted_iota(jnp.int32, (8, tokens), 1) // BLK + first_block
    chosen = block_of == picks_ref[0, 0]
    for i in range(1, picks_ref.shape[1]):
        chosen = chosen | (block_of == picks_ref[0, i])
    chosen_ref[...] = chosen.astype(f32)
    top, rows = ids_ref.shape
    slots = combine_ref.shape[1]
    capacity = weight_ref.shape[0]
    ids = ids_ref[...].T
    expert = lax.broadcasted_iota(jnp.int32, (rows, LANES), 1)
    picked = jnp.zeros((rows, LANES), f32)
    for k in range(top):
        picked = picked + (ids[:, k : k + 1] == expert).astype(f32)
    earlier = lax.broadcasted_iota(jnp.int32, (rows, rows), 1) < lax.broadcasted_iota(
        jnp.int32, (rows, rows), 0
    )
    before = jnp.dot(
        earlier.astype(bf16), picked.astype(bf16), preferred_element_type=f32
    )
    held = jnp.where(picked > 0.5, before, -1.0).astype(bf16)
    spread = lax.broadcasted_iota(jnp.int32, (LANES, slots), 0) == (
        lax.broadcasted_iota(jnp.int32, (LANES, slots), 1) // capacity
    )
    along = jnp.dot(held, spread.astype(bf16), preferred_element_type=f32)
    slot = lax.broadcasted_iota(jnp.int32, (rows, slots), 1) % capacity
    combine_ref[...] = (along == slot.astype(f32)).astype(bf16)
    spread = lax.broadcasted_iota(jnp.int32, (slots, LANES), 1) == (
        lax.broadcasted_iota(jnp.int32, (slots, LANES), 0) // capacity
    )
    down = lax.dot_general(
        spread.astype(bf16), held, (((1,), (1,)), ((), ())), preferred_element_type=f32
    )
    slot = lax.broadcasted_iota(jnp.int32, (slots, rows), 0) % capacity
    dispatch_ref[...] = (down == slot.astype(f32)).astype(bf16)
    here = lax.axis_index("expert")
    weight = jnp.sum(jnp.where(ids == here, gw_ref[...].T, 0.0), axis=1, keepdims=True)
    mine = jnp.sum(
        jnp.where(expert == here, held.astype(f32), 0.0), axis=1, keepdims=True
    )
    by_slot = jnp.sum(jnp.where(mine == expert.astype(f32), weight, 0.0), axis=0, keepdims=True)
    by_slot = jnp.broadcast_to(by_slot, (capacity, LANES))
    diagonal = lax.broadcasted_iota(jnp.int32, (capacity, LANES), 1) == lax.broadcasted_iota(
        jnp.int32, (capacity, LANES), 0
    )
    by_slot = jnp.sum(jnp.where(diagonal, by_slot, 0.0), axis=1, keepdims=True)
    weight_ref[...] = jnp.broadcast_to(by_slot, weight_ref.shape)
    width = residual_ref.shape[1]
    residual_out[...] = jnp.concatenate(
        [residual_ref[...].astype(f32), jnp.zeros((rows, LANES - width), f32)], axis=1
    )
    gain = jnp.concatenate(
        [gain_ref[...].astype(f32), jnp.zeros((1, LANES - width), f32)], axis=1
    )
    gain_out[...] = jnp.broadcast_to(gain, gain_out.shape)


def values_body(parts_ref, uv_ref, out_ref):
    parts = parts_ref[...].astype(f32)
    heads = parts.shape[1]
    stats = parts[:, :, LAT:]
    scale = stats[:, :, 0:1] + stats[:, :, 1:2]
    total = stats[:, :, 2:3] + stats[:, :, 3:4]
    factor = jnp.exp(scale - jnp.max(scale, axis=0, keepdims=True))
    denominator = jnp.sum(factor * total, axis=0)
    attended = jnp.sum(factor * parts[:, :, :LAT], axis=0) / denominator
    row = lax.broadcasted_iota(jnp.int32, attended.shape, 0)
    spread = jnp.concatenate(
        [jnp.where(row == j, attended, 0.0).astype(bf16) for j in range(heads)], axis=1
    )
    head_vals = jnp.dot(spread, uv_ref[...], preferred_element_type=f32).astype(bf16)
    out_ref[...] = jnp.broadcast_to(head_vals[None], out_ref.shape)


def project_body(vals_ref, o_ref, out_ref):
    vals = vals_ref[...].astype(f32)
    wide = jnp.concatenate([vals[:, j, :] for j in range(vals.shape[1])], axis=1).astype(bf16)
    part = jnp.dot(wide, o_ref[...], preferred_element_type=f32).astype(bf16)
    part = jnp.concatenate(
        [part, jnp.zeros((part.shape[0], LANES - part.shape[1]), bf16)], axis=1
    )
    out_ref[...] = jnp.broadcast_to(part[None], out_ref.shape)


def mix_body(width, parts_ref, residual_ref, gain_ref, dispatch_ref, out_ref, mixed_ref):
    attn = jnp.sum(parts_ref[...].astype(f32), axis=0)
    mixed = (residual_ref[...] + attn).astype(bf16).astype(f32)
    mixed_ref[...] = mixed
    squares = jnp.sum(mixed * mixed, axis=1, keepdims=True)
    top = squares.astype(bf16).astype(f32)
    lane = lax.broadcasted_iota(jnp.int32, mixed.shape, 1)
    scaled = jnp.where(
        lane == width, top, jnp.where(lane == width + 1, squares - top, mixed * gain_ref[0:1])
    )
    slots = jnp.dot(dispatch_ref[...], scaled.astype(bf16), preferred_element_type=f32)
    out_ref[...] = slots.astype(bf16).reshape(out_ref.shape)


def expert_body(slots_ref, gate_ref, up_ref, down_ref, weight_ref, out_ref):
    owners, capacity = slots_ref.shape[:2]
    features, units = gate_ref.shape
    width = features // owners
    lane = lax.broadcasted_iota(jnp.int32, (capacity, LANES), 1)
    stats = jnp.sum(slots_ref[...].astype(f32), axis=0)
    stats = jnp.where((lane == width) | (lane == width + 1), stats, 0.0)
    scale = lax.rsqrt(jnp.sum(stats, axis=1, keepdims=True) / features + norm_eps)
    both = jnp.zeros((capacity, 2 * units), f32)
    for i in range(owners):
        part = slice(i * width, (i + 1) * width)
        weights = jnp.concatenate([gate_ref[part, :], up_ref[part, :]], axis=1)
        both += jnp.dot(slots_ref[i][:, :width], weights, preferred_element_type=f32)
    both = both * scale
    gate_act, up_act = both[:, :units], both[:, units:]
    hidden = (gate_act / (1.0 + jnp.exp(-gate_act)) * up_act).astype(bf16)
    outcome = jnp.dot(hidden, down_ref[...], preferred_element_type=f32) * weight_ref[:, 0:1]
    pad = jnp.zeros((capacity, LANES - width), f32)
    for i in range(owners):
        out_ref[i] = jnp.concatenate(
            [outcome[:, i * width : (i + 1) * width], pad], axis=1
        ).astype(bf16)


def gather_body(parts_ref, combine_ref, mixed_ref, out_ref):
    parts = parts_ref[...].reshape(combine_ref.shape[1], LANES)
    share = jnp.dot(combine_ref[...], parts, preferred_element_type=f32)
    share = share + jnp.where(lax.axis_index("head") == 0, mixed_ref[...], 0.0)
    groups, rows = out_ref.shape[0], share.shape[0]
    for i in range(groups):
        group = i * rows // groups // 8
        out_ref[i] = share[group * 8 : group * 8 + 8]


def finish_body(parts_ref, out_ref):
    share = jnp.sum(parts_ref[...], axis=0)
    rows, columns = out_ref.shape
    place = lax.axis_index("head") % (8 // rows)
    mine = share[:rows]
    for i in range(1, 8 // rows):
        mine = jnp.where(place == i, share[i * rows : (i + 1) * rows], mine)
    out_ref[...] = mine[:, :columns].astype(bf16)


def local(
    queries,
    kv_cache,
    block_ids,
    w_uv,
    o_proj,
    residual,
    moe_gain,
    w_gate,
    w_up,
    w_down,
    expert_ids,
    gate_weights,
):
    head_n = lax.axis_size("head")
    expert_n = lax.axis_size("expert")
    heads, width = queries.shape[1:]
    rows, top = expert_ids.shape
    columns = o_proj.shape[1]
    row_share = rows // head_n
    capacity = min(2 * (rows // expert_n) * top, rows)
    slots = expert_n * capacity

    asked = call(copies_body, shape((head_n, heads, width), bf16), [VM], queries)
    asked = exchange(asked, "head")
    tokens = kv_cache.shape[1]
    staged = pl.pallas_call(
        stage_body,
        out_shape=(
            shape((slots, rows), bf16),
            shape((rows, slots), bf16),
            shape((capacity, LANES), f32),
            shape((rows, LANES), f32),
            shape((8, LANES), f32),
            shape((8, tokens), f32),
            shape(o_proj.shape, bf16),
            shape((width, tokens), bf16),
        ),
        in_specs=[pl.BlockSpec(memory_space=pl.ANY)] * 7,
        out_specs=(VM,) * 8,
        scratch_shapes=[
            pltpu.VMEM((top, rows), jnp.int32),
            pltpu.VMEM((top, rows), f32),
            pltpu.VMEM((rows, columns), bf16),
            pltpu.VMEM((1, columns), bf16),
            pltpu.SMEM(block_ids.shape, jnp.int32),
            pltpu.VMEM((columns, o_proj.shape[0]), bf16),
            pltpu.SemaphoreType.DMA((7,)),
        ],
        compiler_params=pltpu.CompilerParams(vmem_limit_bytes=48 * 1024 * 1024),
    )(
        expert_ids.T,
        gate_weights.T,
        residual,
        moe_gain[None, :],
        block_ids,
        o_proj.T,
        kv_cache[0].T,
    )
    staged, asked = lax.optimization_barrier((staged, asked))
    dispatch, combine, weight, residual_wide, gain, chosen, o_proj, cache = staged
    shares = call(
        attend_body,
        shape((head_n * heads, LAT + LANES), bf16),
        [VM] * 3,
        chosen,
        asked.reshape(head_n * heads, width),
        cache,
    )
    shares = exchange(shares.reshape(head_n, heads, LAT + LANES), "head")
    vals = call(
        values_body,
        shape((expert_n, heads, w_uv.shape[2]), bf16),
        [VM, VM],
        shares,
        w_uv.reshape(heads * LAT, -1),
    )
    vals = exchange(vals, "expert")
    attn = call(project_body, shape((head_n, rows, LANES), bf16), [VM, VM], vals, o_proj)
    attn = exchange(attn, "head")
    tokens, mixed = call(
        functools.partial(mix_body, columns),
        (shape((expert_n, capacity, LANES), bf16), shape((rows, LANES), f32)),
        [VM] * 4,
        attn,
        residual_wide,
        gain,
        dispatch,
    )
    tokens = exchange(tokens, "expert")
    outcome = call(
        expert_body,
        shape((expert_n, capacity, LANES), bf16),
        [VM] * 5,
        tokens,
        w_gate[0],
        w_up[0],
        w_down[0],
        weight,
    )
    outcome = exchange(outcome, "expert")
    moe = call(gather_body, shape((head_n, 8, LANES), f32), [VM] * 3, outcome, combine, mixed)
    return call(finish_body, shape((row_share, columns), bf16), [VM], exchange(moe, "head"))


def solution(mesh):
    in_specs = (
        P("expert", "head", None),
        P("expert", "head", None),
        P("expert", None),
        P("head", None, None),
        P("head", "expert"),
        P(None, "expert"),
        P("expert"),
        P("expert", None, "head"),
        P("expert", None, "head"),
        P("expert", "head", None),
        P(),
        P(),
    )
    out_specs = P("head", "expert")
    return jax.shard_map(local, mesh=mesh, in_specs=in_specs, out_specs=out_specs, check_vma=False)
```

```python
import functools

import jax
import jax.numpy as jnp
from jax import lax
from jax.experimental import pallas as pl
from jax.experimental.pallas import tpu as pltpu
from jax.sharding import PartitionSpec as P

LAT = 512
BLK = 64
LANES = 128
NEG = -1e30

score_scale = 192 ** (-0.5)
norm_eps = 1e-06

f32 = jnp.float32
bf16 = jnp.bfloat16


VM = pl.BlockSpec(memory_space=pltpu.VMEM)
SM = pl.BlockSpec(memory_space=pltpu.SMEM)
shape = jax.ShapeDtypeStruct


def call(body, out_shape, in_specs, *operands):
    return pl.pallas_call(
        body,
        out_shape=out_shape,
        in_specs=in_specs,
        out_specs=jax.tree.map(lambda _: VM, out_shape),
        compiler_params=pltpu.CompilerParams(vmem_limit_bytes=48 * 1024 * 1024),
    )(*operands)


def ring(axis, count):
    first = count // 2 + 1 if axis == "head" else count * 5 // 8
    return [(first + i) % count for i in range(count)]


def exchange(blocks, axis):
    groups = [ring(axis, blocks.shape[0])]
    return lax.all_to_all(
        blocks, axis, split_axis=0, concat_axis=0, tiled=True, axis_index_groups=groups
    )


def attend_body(chosen_ref, q_ref, kv_ref, out_ref):
    chosen = chosen_ref[0:1] > 0.5
    scores = (
        jnp.dot(q_ref[...], kv_ref[...], preferred_element_type=f32) * score_scale
    )
    scores = jnp.where(chosen, scores, NEG)
    highest = jnp.max(scores, axis=1, keepdims=True)
    top = highest.astype(bf16).astype(f32)
    rest = (highest - top).astype(bf16).astype(f32)
    weights = jnp.where(chosen, jnp.exp(scores - (top + rest)), 0.0)
    total = jnp.sum(weights, axis=1, keepdims=True)
    latent = lax.dot_general(
        weights.astype(bf16), kv_ref[:LAT, :], (((1,), (1,)), ((), ())), preferred_element_type=f32
    )
    total_top = total.astype(bf16).astype(f32)
    total_rest = total - total_top
    lane = lax.broadcasted_iota(jnp.int32, (q_ref.shape[0], LANES), 1)
    stats = jnp.where(
        lane == 0, top, jnp.where(lane == 1, rest, jnp.where(lane == 2, total_top, total_rest))
    )
    out_ref[:, :LAT] = latent.astype(bf16)
    out_ref[:, LAT:] = stats.astype(bf16)


def stage_body(
    queries_any, ids_any, gw_any, residual_any, gain_any, picks_any, o_any, cache_any,
    copies_out, dispatch_ref, combine_ref, weight_ref, residual_out, gain_out, chosen_ref, o_out, cache_out,
    query_ref, ids_ref, gw_ref, residual_ref, gain_ref, picks_ref, o_ref, sems,
):
    pairs = (
        (queries_any, query_ref),
        (ids_any, ids_ref),
        (gw_any, gw_ref),
        (residual_any, residual_ref),
        (gain_any, gain_ref),
        (picks_any, picks_ref),
        (o_any, o_ref),
        (cache_any, cache_out),
    )
    copies = [pltpu.make_async_copy(a, b, sems.at[i]) for i, (a, b) in enumerate(pairs)]
    for copy in copies:
        copy.start()
    for copy in copies[:-2]:
        copy.wait()
    copies_out[...] = jnp.broadcast_to(query_ref[...], copies_out.shape)
    tokens = chosen_ref.shape[1]
    first_block = lax.axis_index("head") * (tokens // BLK)
    block_of = lax.broadcasted_iota(jnp.int32, (8, tokens), 1) // BLK + first_block
    chosen = block_of == picks_ref[0, 0]
    for i in range(1, picks_ref.shape[1]):
        chosen = chosen | (block_of == picks_ref[0, i])
    chosen_ref[...] = chosen.astype(f32)
    top, rows = ids_ref.shape
    slots = combine_ref.shape[1]
    capacity = weight_ref.shape[0]
    ids = ids_ref[...].T
    expert = lax.broadcasted_iota(jnp.int32, (rows, LANES), 1)
    picked = jnp.zeros((rows, LANES), f32)
    for k in range(top):
        picked = picked + (ids[:, k : k + 1] == expert).astype(f32)
    earlier = lax.broadcasted_iota(jnp.int32, (rows, rows), 1) < lax.broadcasted_iota(
        jnp.int32, (rows, rows), 0
    )
    before = jnp.dot(
        earlier.astype(bf16), picked.astype(bf16), preferred_element_type=f32
    )
    held = jnp.where(picked > 0.5, before, -1.0).astype(bf16)
    spread = lax.broadcasted_iota(jnp.int32, (LANES, slots), 0) == (
        lax.broadcasted_iota(jnp.int32, (LANES, slots), 1) // capacity
    )
    along = jnp.dot(held, spread.astype(bf16), preferred_element_type=f32)
    slot = lax.broadcasted_iota(jnp.int32, (rows, slots), 1) % capacity
    combine_ref[...] = (along == slot.astype(f32)).astype(bf16)
    spread = lax.broadcasted_iota(jnp.int32, (slots, LANES), 1) == (
        lax.broadcasted_iota(jnp.int32, (slots, LANES), 0) // capacity
    )
    down = lax.dot_general(
        spread.astype(bf16), held, (((1,), (1,)), ((), ())), preferred_element_type=f32
    )
    slot = lax.broadcasted_iota(jnp.int32, (slots, rows), 0) % capacity
    dispatch_ref[...] = (down == slot.astype(f32)).astype(bf16)
    here = lax.axis_index("expert")
    weight = jnp.sum(jnp.where(ids == here, gw_ref[...].T, 0.0), axis=1, keepdims=True)
    mine = jnp.sum(
        jnp.where(expert == here, held.astype(f32), 0.0), axis=1, keepdims=True
    )
    by_slot = jnp.sum(jnp.where(mine == expert.astype(f32), weight, 0.0), axis=0, keepdims=True)
    by_slot = jnp.broadcast_to(by_slot, (capacity, LANES))
    diagonal = lax.broadcasted_iota(jnp.int32, (capacity, LANES), 1) == lax.broadcasted_iota(
        jnp.int32, (capacity, LANES), 0
    )
    by_slot = jnp.sum(jnp.where(diagonal, by_slot, 0.0), axis=1, keepdims=True)
    weight_ref[...] = jnp.broadcast_to(by_slot, weight_ref.shape)
    width = residual_ref.shape[1]
    residual_out[...] = jnp.concatenate(
        [residual_ref[...].astype(f32), jnp.zeros((rows, LANES - width), f32)], axis=1
    )
    gain = jnp.concatenate(
        [gain_ref[...].astype(f32), jnp.zeros((1, LANES - width), f32)], axis=1
    )
    gain_out[...] = jnp.broadcast_to(gain, gain_out.shape)
    for copy in copies[-2:]:
        copy.wait()
    o_out[...] = o_ref[...].T


def values_body(parts_ref, uv_ref, out_ref):
    parts = parts_ref[...].astype(f32)
    heads = parts.shape[1]
    stats = parts[:, :, LAT:]
    scale = stats[:, :, 0:1] + stats[:, :, 1:2]
    total = stats[:, :, 2:3] + stats[:, :, 3:4]
    factor = jnp.exp(scale - jnp.max(scale, axis=0, keepdims=True))
    denominator = jnp.sum(factor * total, axis=0)
    attended = jnp.sum(factor * parts[:, :, :LAT], axis=0) / denominator
    row = lax.broadcasted_iota(jnp.int32, attended.shape, 0)
    spread = jnp.concatenate(
        [jnp.where(row == j, attended, 0.0).astype(bf16) for j in range(heads)], axis=1
    )
    head_vals = jnp.dot(spread, uv_ref[...], preferred_element_type=f32).astype(bf16)
    out_ref[...] = jnp.broadcast_to(head_vals[None], out_ref.shape)


def project_body(vals_ref, o_ref, out_ref):
    order = ring("expert", vals_ref.shape[0])
    vals = jnp.stack([vals_ref[order.index(i)] for i in range(len(order))]).astype(f32)
    wide = jnp.concatenate([vals[:, j, :] for j in range(vals.shape[1])], axis=1).astype(bf16)
    part = jnp.dot(wide, o_ref[...], preferred_element_type=f32).astype(bf16)
    part = jnp.concatenate(
        [part, jnp.zeros((part.shape[0], LANES - part.shape[1]), bf16)], axis=1
    )
    out_ref[...] = jnp.broadcast_to(part[None], out_ref.shape)


def mix_body(width, parts_ref, residual_ref, gain_ref, dispatch_ref, out_ref, mixed_ref):
    attn = jnp.sum(parts_ref[...].astype(f32), axis=0)
    mixed = (residual_ref[...] + attn).astype(bf16).astype(f32)
    mixed_ref[...] = mixed
    squares = jnp.sum(mixed * mixed, axis=1, keepdims=True)
    top = squares.astype(bf16).astype(f32)
    lane = lax.broadcasted_iota(jnp.int32, mixed.shape, 1)
    scaled = jnp.where(
        lane == width, top, jnp.where(lane == width + 1, squares - top, mixed * gain_ref[0:1])
    )
    slots = jnp.dot(dispatch_ref[...], scaled.astype(bf16), preferred_element_type=f32)
    slots = slots.astype(bf16).reshape(out_ref.shape)
    for i, expert in enumerate(ring("expert", out_ref.shape[0])):
        out_ref[i] = slots[expert]


def expert_body(slots_ref, gate_ref, up_ref, down_ref, weight_ref, out_ref):
    owners, capacity = slots_ref.shape[:2]
    features, units = gate_ref.shape
    width = features // owners
    lane = lax.broadcasted_iota(jnp.int32, (capacity, LANES), 1)
    stats = jnp.sum(slots_ref[...].astype(f32), axis=0)
    stats = jnp.where((lane == width) | (lane == width + 1), stats, 0.0)
    scale = lax.rsqrt(jnp.sum(stats, axis=1, keepdims=True) / features + norm_eps)
    both = jnp.zeros((capacity, 2 * units), f32)
    order = ring("expert", owners)
    for i, owner in enumerate(order):
        part = slice(owner * width, (owner + 1) * width)
        weights = jnp.concatenate([gate_ref[part, :], up_ref[part, :]], axis=1)
        both += jnp.dot(slots_ref[i][:, :width], weights, preferred_element_type=f32)
    both = both * scale
    gate_act, up_act = both[:, :units], both[:, units:]
    hidden = (gate_act / (1.0 + jnp.exp(-gate_act)) * up_act).astype(bf16)
    outcome = jnp.dot(hidden, down_ref[...], preferred_element_type=f32) * weight_ref[:, 0:1]
    pad = jnp.zeros((capacity, LANES - width), f32)
    for i, owner in enumerate(order):
        out_ref[i] = jnp.concatenate(
            [outcome[:, owner * width : (owner + 1) * width], pad], axis=1
        ).astype(bf16)


def gather_body(parts_ref, combine_ref, mixed_ref, out_ref):
    order = ring("expert", parts_ref.shape[0])
    parts = jnp.stack([parts_ref[order.index(i)] for i in range(len(order))])
    parts = parts.reshape(combine_ref.shape[1], LANES)
    share = jnp.dot(combine_ref[...], parts, preferred_element_type=f32)
    share = share + jnp.where(lax.axis_index("head") == 0, mixed_ref[...], 0.0)
    groups, rows = out_ref.shape[0], share.shape[0]
    for i, owner in enumerate(ring("head", groups)):
        group = owner * rows // groups // 8
        out_ref[i] = share[group * 8 : group * 8 + 8]


def finish_body(parts_ref, out_ref):
    share = jnp.sum(parts_ref[...], axis=0)
    rows, columns = out_ref.shape
    place = lax.axis_index("head") % (8 // rows)
    mine = share[:rows]
    for i in range(1, 8 // rows):
        mine = jnp.where(place == i, share[i * rows : (i + 1) * rows], mine)
    out_ref[...] = mine[:, :columns].astype(bf16)


def local(
    queries,
    kv_cache,
    block_ids,
    w_uv,
    o_proj,
    residual,
    moe_gain,
    w_gate,
    w_up,
    w_down,
    expert_ids,
    gate_weights,
):
    head_n = lax.axis_size("head")
    expert_n = lax.axis_size("expert")
    heads, width = queries.shape[1:]
    rows, top = expert_ids.shape
    columns = o_proj.shape[1]
    row_share = rows // head_n
    capacity = min(2 * (rows // expert_n) * top, rows)
    slots = expert_n * capacity

    tokens = kv_cache.shape[1]
    staged = pl.pallas_call(
        stage_body,
        out_shape=(
            shape((head_n, heads, width), bf16),
            shape((slots, rows), bf16),
            shape((rows, slots), bf16),
            shape((capacity, LANES), f32),
            shape((rows, LANES), f32),
            shape((8, LANES), f32),
            shape((8, tokens), f32),
            shape(o_proj.shape, bf16),
            shape((width, tokens), bf16),
        ),
        in_specs=[pl.BlockSpec(memory_space=pltpu.HBM)] * 8,
        out_specs=(VM,) * 9,
        scratch_shapes=[
            pltpu.VMEM(queries.shape, bf16),
            pltpu.VMEM((top, rows), jnp.int32),
            pltpu.VMEM((top, rows), f32),
            pltpu.VMEM((rows, columns), bf16),
            pltpu.VMEM((1, columns), bf16),
            pltpu.SMEM(block_ids.shape, jnp.int32),
            pltpu.VMEM((columns, o_proj.shape[0]), bf16),
            pltpu.SemaphoreType.DMA((8,)),
        ],
        compiler_params=pltpu.CompilerParams(vmem_limit_bytes=48 * 1024 * 1024),
    )(
        *(
            pltpu.with_memory_space_constraint(array, pltpu.HBM)
            for array in (
                queries,
                expert_ids.T,
                gate_weights.T,
                residual,
                moe_gain[None, :],
                block_ids,
                o_proj.T,
                kv_cache[0].T,
            )
        )
    )
    asked, dispatch, combine, weight, residual_wide, gain, chosen, o_proj, cache = staged
    asked = exchange(asked, "head")
    shares = call(
        attend_body,
        shape((head_n * heads, LAT + LANES), bf16),
        [VM] * 3,
        chosen,
        asked.reshape(head_n * heads, width),
        cache,
    )
    shares = exchange(shares.reshape(head_n, heads, LAT + LANES), "head")
    vals = call(
        values_body,
        shape((expert_n, heads, w_uv.shape[2]), bf16),
        [VM, VM],
        shares,
        w_uv.reshape(heads * LAT, -1),
    )
    vals = exchange(vals, "expert")
    attn = call(project_body, shape((head_n, rows, LANES), bf16), [VM, VM], vals, o_proj)
    attn = exchange(attn, "head")
    tokens, mixed = call(
        functools.partial(mix_body, columns),
        (shape((expert_n, capacity, LANES), bf16), shape((rows, LANES), f32)),
        [VM] * 4,
        attn,
        residual_wide,
        gain,
        dispatch,
    )
    tokens = exchange(tokens, "expert")
    outcome = call(
        expert_body,
        shape((expert_n, capacity, LANES), bf16),
        [VM] * 5,
        tokens,
        w_gate[0],
        w_up[0],
        w_down[0],
        weight,
    )
    outcome = exchange(outcome, "expert")
    moe = call(gather_body, shape((head_n, 8, LANES), f32), [VM] * 3, outcome, combine, mixed)
    return call(finish_body, shape((row_share, columns), bf16), [VM], exchange(moe, "head"))


def solution(mesh):
    in_specs = (
        P("expert", "head", None),
        P("expert", "head", None),
        P("expert", None),
        P("head", None, None),
        P("head", "expert"),
        P(None, "expert"),
        P("expert"),
        P("expert", None, "head"),
        P("expert", None, "head"),
        P("expert", "head", None),
        P(),
        P(),
    )
    out_specs = P("head", "expert")
    return jax.shard_map(local, mesh=mesh, in_specs=in_specs, out_specs=out_specs, check_vma=False)
```

```python
import functools

import jax
import jax.numpy as jnp
from jax import lax
from jax.experimental import pallas as pl
from jax.experimental.pallas import tpu as pltpu
from jax.sharding import PartitionSpec as P

LAT = 512
BLK = 64
LANES = 128
NEG = -1e30

score_scale = 192 ** (-0.5)
norm_eps = 1e-06

f32 = jnp.float32
bf16 = jnp.bfloat16


VM = pl.BlockSpec(memory_space=pltpu.VMEM)
SM = pl.BlockSpec(memory_space=pltpu.SMEM)
shape = jax.ShapeDtypeStruct


def call(body, out_shape, in_specs, *operands):
    return pl.pallas_call(
        body,
        out_shape=out_shape,
        in_specs=in_specs,
        out_specs=jax.tree.map(lambda _: VM, out_shape),
        compiler_params=pltpu.CompilerParams(vmem_limit_bytes=48 * 1024 * 1024),
    )(*operands)


def ring(axis, count):
    first = count // 2 + 1 if axis == "head" else count * 5 // 8
    return [(first + i) % count for i in range(count)]


def exchange(blocks, axis):
    groups = [ring(axis, blocks.shape[0])]
    return lax.all_to_all(
        blocks, axis, split_axis=0, concat_axis=0, tiled=True, axis_index_groups=groups
    )


def attend_body(chosen_ref, q_ref, kv_ref, out_ref):
    chosen = chosen_ref[0:1] > 0.5
    scores = (
        jnp.dot(q_ref[...], kv_ref[...], preferred_element_type=f32) * score_scale
    )
    scores = jnp.where(chosen, scores, NEG)
    highest = jnp.max(scores, axis=1, keepdims=True)
    top = highest.astype(bf16).astype(f32)
    rest = (highest - top).astype(bf16).astype(f32)
    weights = jnp.where(chosen, jnp.exp(scores - (top + rest)), 0.0)
    total = jnp.sum(weights, axis=1, keepdims=True)
    latent = lax.dot_general(
        weights.astype(bf16), kv_ref[:LAT, :], (((1,), (1,)), ((), ())), preferred_element_type=f32
    )
    total_top = total.astype(bf16).astype(f32)
    total_rest = total - total_top
    lane = lax.broadcasted_iota(jnp.int32, (q_ref.shape[0], LANES), 1)
    stats = jnp.where(
        lane == 0, top, jnp.where(lane == 1, rest, jnp.where(lane == 2, total_top, total_rest))
    )
    out_ref[:, :LAT] = latent.astype(bf16)
    out_ref[:, LAT:] = stats.astype(bf16)


def stage_body(
    queries_any, ids_any, gw_any, residual_any, gain_any, picks_any, o_any, cache_any,
    copies_out, dispatch_ref, combine_ref, weight_ref, residual_out, gain_out, chosen_ref, o_out, cache_out,
    query_ref, ids_ref, gw_ref, residual_ref, gain_ref, picks_ref, o_ref, sems,
):
    pairs = (
        (queries_any, query_ref),
        (ids_any, ids_ref),
        (gw_any, gw_ref),
        (residual_any, residual_ref),
        (gain_any, gain_ref),
        (picks_any, picks_ref),
        (o_any, o_ref),
        (cache_any, cache_out),
    )
    copies = [pltpu.make_async_copy(a, b, sems.at[i]) for i, (a, b) in enumerate(pairs)]
    for copy in copies:
        copy.start()
    top, rows = ids_ref.shape
    slots = combine_ref.shape[1]
    capacity = weight_ref.shape[0]
    experts = slots // capacity
    expert = lax.broadcasted_iota(jnp.int32, (experts, rows), 0)
    earlier = lax.broadcasted_iota(jnp.int32, (rows, rows), 0) < lax.broadcasted_iota(
        jnp.int32, (rows, rows), 1
    )
    earlier = earlier.astype(bf16)
    for copy in copies[:-2]:
        copy.wait()
    copies_out[...] = jnp.broadcast_to(query_ref[...], copies_out.shape)
    tokens = chosen_ref.shape[1]
    first_block = lax.axis_index("head") * (tokens // BLK)
    block_of = lax.broadcasted_iota(jnp.int32, (1, tokens), 1) // BLK + first_block
    count = picks_ref.shape[1]
    diagonal = lax.broadcasted_iota(jnp.int32, (count, count), 0) == lax.broadcasted_iota(
        jnp.int32, (count, count), 1
    )
    picks = jnp.sum(jnp.where(diagonal, picks_ref[...], 0), axis=1, keepdims=True)
    chosen = jnp.max((block_of == picks).astype(f32), axis=0, keepdims=True)
    chosen_ref[...] = jnp.broadcast_to(chosen, chosen_ref.shape)
    ids = ids_ref[...]
    picked = jnp.zeros((experts, rows), f32)
    for k in range(top):
        picked = picked + (ids[k : k + 1, :] == expert).astype(f32)
    before = jnp.dot(picked.astype(bf16), earlier, preferred_element_type=f32)
    held = jnp.where(picked > 0.5, before, -1.0)
    slot = lax.broadcasted_iota(jnp.int32, (experts, capacity, rows), 1).astype(f32)
    dispatch = (held[:, None, :] == slot).astype(f32).reshape(slots, rows)
    dispatch_ref[...] = dispatch.astype(bf16)
    combine_ref[...] = dispatch.T.astype(bf16)
    here = lax.axis_index("expert")
    weight = jnp.sum(jnp.where(ids == here, gw_ref[...], 0.0), axis=0, keepdims=True)
    mine = jnp.sum(jnp.where(expert == here, held, 0.0), axis=0, keepdims=True)
    slot = lax.broadcasted_iota(jnp.int32, (capacity, rows), 0).astype(f32)
    weight = jnp.sum(jnp.where(mine == slot, weight, 0.0), axis=1, keepdims=True)
    weight_ref[...] = jnp.broadcast_to(weight, weight_ref.shape)
    width = residual_ref.shape[1]
    residual_out[...] = jnp.concatenate(
        [residual_ref[...].astype(f32), jnp.zeros((rows, LANES - width), f32)], axis=1
    )
    gain = jnp.concatenate(
        [gain_ref[...].astype(f32), jnp.zeros((1, LANES - width), f32)], axis=1
    )
    gain_out[...] = jnp.broadcast_to(gain, gain_out.shape)
    for copy in copies[-2:]:
        copy.wait()
    o_out[...] = o_ref[...]


def values_body(parts_ref, uv_ref, out_ref):
    parts = parts_ref[...].astype(f32)
    heads = parts.shape[1]
    stats = parts[:, :, LAT:]
    scale = stats[:, :, 0:1] + stats[:, :, 1:2]
    total = stats[:, :, 2:3] + stats[:, :, 3:4]
    factor = jnp.exp(scale - jnp.max(scale, axis=0, keepdims=True))
    denominator = jnp.sum(factor * total, axis=0)
    attended = jnp.sum(factor * parts[:, :, :LAT], axis=0) / denominator
    row = lax.broadcasted_iota(jnp.int32, attended.shape, 0)
    spread = jnp.concatenate(
        [jnp.where(row == j, attended, 0.0).astype(bf16) for j in range(heads)], axis=1
    )
    head_vals = jnp.dot(spread, uv_ref[...], preferred_element_type=f32).astype(bf16)
    out_ref[...] = jnp.broadcast_to(head_vals[None], out_ref.shape)


def project_body(vals_ref, o_ref, out_ref):
    order = ring("expert", vals_ref.shape[0])
    vals = jnp.stack([vals_ref[order.index(i)] for i in range(len(order))]).astype(f32)
    wide = jnp.concatenate([vals[:, j, :] for j in range(vals.shape[1])], axis=1).astype(bf16)
    part = lax.dot_general(
        wide, o_ref[...], (((1,), (1,)), ((), ())), preferred_element_type=f32
    ).astype(bf16)
    part = jnp.concatenate(
        [part, jnp.zeros((part.shape[0], LANES - part.shape[1]), bf16)], axis=1
    )
    out_ref[...] = jnp.broadcast_to(part[None], out_ref.shape)


def mix_body(width, parts_ref, residual_ref, gain_ref, dispatch_ref, out_ref, mixed_ref):
    attn = jnp.sum(parts_ref[...].astype(f32), axis=0)
    mixed = (residual_ref[...] + attn).astype(bf16).astype(f32)
    mixed_ref[...] = mixed
    squares = jnp.sum(mixed * mixed, axis=1, keepdims=True)
    top = squares.astype(bf16).astype(f32)
    lane = lax.broadcasted_iota(jnp.int32, mixed.shape, 1)
    scaled = jnp.where(
        lane == width, top, jnp.where(lane == width + 1, squares - top, mixed * gain_ref[0:1])
    )
    slots = jnp.dot(dispatch_ref[...], scaled.astype(bf16), preferred_element_type=f32)
    slots = slots.astype(bf16).reshape(out_ref.shape)
    for i, expert in enumerate(ring("expert", out_ref.shape[0])):
        out_ref[i] = slots[expert]


def expert_body(slots_ref, gate_ref, up_ref, down_ref, weight_ref, out_ref):
    owners, capacity = slots_ref.shape[:2]
    features, units = gate_ref.shape
    width = features // owners
    lane = lax.broadcasted_iota(jnp.int32, (capacity, LANES), 1)
    stats = jnp.sum(slots_ref[...].astype(f32), axis=0)
    stats = jnp.where((lane == width) | (lane == width + 1), stats, 0.0)
    scale = lax.rsqrt(jnp.sum(stats, axis=1, keepdims=True) / features + norm_eps)
    order = ring("expert", owners)
    wide = jnp.concatenate(
        [slots_ref[order.index(i)][:, :width] for i in range(owners)], axis=1
    )
    gate_act = jnp.dot(wide, gate_ref[...], preferred_element_type=f32) * scale
    up_act = jnp.dot(wide, up_ref[...], preferred_element_type=f32) * scale
    hidden = (gate_act / (1.0 + jnp.exp(-gate_act)) * up_act).astype(bf16)
    outcome = jnp.dot(hidden, down_ref[...], preferred_element_type=f32) * weight_ref[:, 0:1]
    pad = jnp.zeros((capacity, LANES - width), f32)
    for i, owner in enumerate(order):
        out_ref[i] = jnp.concatenate(
            [outcome[:, owner * width : (owner + 1) * width], pad], axis=1
        ).astype(bf16)


def gather_body(parts_ref, combine_ref, mixed_ref, out_ref):
    order = ring("expert", parts_ref.shape[0])
    parts = jnp.stack([parts_ref[order.index(i)] for i in range(len(order))])
    parts = parts.reshape(combine_ref.shape[1], LANES)
    share = jnp.dot(combine_ref[...], parts, preferred_element_type=f32)
    share = share + jnp.where(lax.axis_index("head") == 0, mixed_ref[...], 0.0)
    groups, rows = out_ref.shape[0], share.shape[0]
    for i, owner in enumerate(ring("head", groups)):
        group = owner * rows // groups // 8
        out_ref[i] = share[group * 8 : group * 8 + 8]


def finish_body(parts_ref, out_ref):
    share = jnp.sum(parts_ref[...], axis=0)
    rows, columns = out_ref.shape
    place = lax.axis_index("head") % (8 // rows)
    mine = share[:rows]
    for i in range(1, 8 // rows):
        mine = jnp.where(place == i, share[i * rows : (i + 1) * rows], mine)
    out_ref[...] = mine[:, :columns].astype(bf16)


def local(
    queries,
    kv_cache,
    block_ids,
    w_uv,
    o_proj,
    residual,
    moe_gain,
    w_gate,
    w_up,
    w_down,
    expert_ids,
    gate_weights,
):
    head_n = lax.axis_size("head")
    expert_n = lax.axis_size("expert")
    heads, width = queries.shape[1:]
    rows, top = expert_ids.shape
    columns = o_proj.shape[1]
    row_share = rows // head_n
    capacity = min(2 * (rows // expert_n) * top, rows)
    slots = expert_n * capacity

    tokens = kv_cache.shape[1]
    staged = pl.pallas_call(
        stage_body,
        out_shape=(
            shape((head_n, heads, width), bf16),
            shape((slots, rows), bf16),
            shape((rows, slots), bf16),
            shape((capacity, LANES), f32),
            shape((rows, LANES), f32),
            shape((8, LANES), f32),
            shape((8, tokens), f32),
            shape(o_proj.shape[::-1], bf16),
            shape((width, tokens), bf16),
        ),
        in_specs=[pl.BlockSpec(memory_space=pltpu.HBM)] * 8,
        out_specs=(VM,) * 9,
        scratch_shapes=[
            pltpu.VMEM(queries.shape, bf16),
            pltpu.VMEM((top, rows), jnp.int32),
            pltpu.VMEM((top, rows), f32),
            pltpu.VMEM((rows, columns), bf16),
            pltpu.VMEM((1, columns), bf16),
            pltpu.VMEM(block_ids.shape, jnp.int32),
            pltpu.VMEM((columns, o_proj.shape[0]), bf16),
            pltpu.SemaphoreType.DMA((8,)),
        ],
        compiler_params=pltpu.CompilerParams(vmem_limit_bytes=48 * 1024 * 1024),
    )(
        *(
            pltpu.with_memory_space_constraint(array, pltpu.HBM)
            for array in (
                queries,
                expert_ids.T,
                gate_weights.T,
                residual,
                moe_gain[None, :],
                block_ids,
                o_proj.T,
                kv_cache[0].T,
            )
        )
    )
    asked, dispatch, combine, weight, residual_wide, gain, chosen, o_proj, cache = staged
    asked = exchange(asked, "head")
    shares = call(
        attend_body,
        shape((head_n * heads, LAT + LANES), bf16),
        [VM] * 3,
        chosen,
        asked.reshape(head_n * heads, width),
        cache,
    )
    shares = exchange(shares.reshape(head_n, heads, LAT + LANES), "head")
    vals = call(
        values_body,
        shape((expert_n, heads, w_uv.shape[2]), bf16),
        [VM, VM],
        shares,
        w_uv.reshape(heads * LAT, -1),
    )
    vals = exchange(vals, "expert")
    attn = call(project_body, shape((head_n, rows, LANES), bf16), [VM, VM], vals, o_proj)
    attn = exchange(attn, "head")
    tokens, mixed = call(
        functools.partial(mix_body, columns),
        (shape((expert_n, capacity, LANES), bf16), shape((rows, LANES), f32)),
        [VM] * 4,
        attn,
        residual_wide,
        gain,
        dispatch,
    )
    tokens = exchange(tokens, "expert")
    outcome = call(
        expert_body,
        shape((expert_n, capacity, LANES), bf16),
        [VM] * 5,
        tokens,
        w_gate[0],
        w_up[0],
        w_down[0],
        weight,
    )
    outcome = exchange(outcome, "expert")
    moe = call(gather_body, shape((head_n, 8, LANES), f32), [VM] * 3, outcome, combine, mixed)
    return call(finish_body, shape((row_share, columns), bf16), [VM], exchange(moe, "head"))


def solution(mesh):
    in_specs = (
        P("expert", "head", None),
        P("expert", "head", None),
        P("expert", None),
        P("head", None, None),
        P("head", "expert"),
        P(None, "expert"),
        P("expert"),
        P("expert", None, "head"),
        P("expert", None, "head"),
        P("expert", "head", None),
        P(),
        P(),
    )
    out_specs = P("head", "expert")
    return jax.shard_map(local, mesh=mesh, in_specs=in_specs, out_specs=out_specs, check_vma=False)
```

```python
import functools

import jax
import jax.numpy as jnp
from jax import lax
from jax.experimental import pallas as pl
from jax.experimental.pallas import tpu as pltpu
from jax.sharding import PartitionSpec as P

LAT = 512
BLK = 64
LANES = 128
NEG = -1e30

score_scale = 192 ** (-0.5)
norm_eps = 1e-06

f32 = jnp.float32
bf16 = jnp.bfloat16


VM = pl.BlockSpec(memory_space=pltpu.VMEM)
SM = pl.BlockSpec(memory_space=pltpu.SMEM)
shape = jax.ShapeDtypeStruct


def call(body, out_shape, in_specs, *operands):
    return pl.pallas_call(
        body,
        out_shape=out_shape,
        in_specs=in_specs,
        out_specs=jax.tree.map(lambda _: VM, out_shape),
        compiler_params=pltpu.CompilerParams(vmem_limit_bytes=48 * 1024 * 1024),
    )(*operands)


def ring(axis, count):
    first = count // 2 + 1 if axis == "head" else count * 5 // 8
    return [(first + i) % count for i in range(count)]


def exchange(blocks, axis, groups=None):
    groups = groups or [ring(axis, blocks.shape[0])]
    return lax.all_to_all(
        blocks, axis, split_axis=0, concat_axis=0, tiled=True, axis_index_groups=groups
    )


def attend_body(chosen_ref, q_ref, mine_ref, other_ref, out_ref):
    caches = (mine_ref, other_ref)
    chosen = chosen_ref[0:1] > 0.5
    scores = jnp.concatenate(
        [jnp.dot(q_ref[...], ref[...], preferred_element_type=f32) for ref in caches], axis=1
    )
    scores = jnp.where(chosen, scores * score_scale, NEG)
    highest = jnp.max(scores, axis=1, keepdims=True)
    top = highest.astype(bf16).astype(f32)
    rest = (highest - top).astype(bf16).astype(f32)
    weights = jnp.where(chosen, jnp.exp(scores - (top + rest)), 0.0)
    total = jnp.sum(weights, axis=1, keepdims=True)
    weights = weights.astype(bf16)
    tokens = mine_ref.shape[1]
    latent = sum(
        lax.dot_general(
            weights[:, i * tokens : (i + 1) * tokens],
            ref[:LAT, :],
            (((1,), (1,)), ((), ())),
            preferred_element_type=f32,
        )
        for i, ref in enumerate(caches)
    )
    total_top = total.astype(bf16).astype(f32)
    total_rest = total - total_top
    lane = lax.broadcasted_iota(jnp.int32, (q_ref.shape[0], LANES), 1)
    stats = jnp.where(
        lane == 0, top, jnp.where(lane == 1, rest, jnp.where(lane == 2, total_top, total_rest))
    )
    out_ref[:, :LAT] = latent.astype(bf16)
    out_ref[:, LAT:] = stats.astype(bf16)


def stage_body(
    queries_any, ids_any, gw_any, residual_any, gain_any, picks_any, o_any, cache_any,
    copies_out, dispatch_ref, combine_ref, weight_ref, residual_out, gain_out, chosen_ref, o_out, cache_out,
    query_ref, ids_ref, gw_ref, residual_ref, gain_ref, picks_ref, o_ref, sems,
):
    pairs = (
        (queries_any, query_ref),
        (ids_any, ids_ref),
        (gw_any, gw_ref),
        (residual_any, residual_ref),
        (gain_any, gain_ref),
        (picks_any, picks_ref),
        (o_any, o_ref),
        (cache_any, cache_out),
    )
    copies = [pltpu.make_async_copy(a, b, sems.at[i]) for i, (a, b) in enumerate(pairs)]
    for copy in copies:
        copy.start()
    top, rows = ids_ref.shape
    slots = combine_ref.shape[1]
    capacity = weight_ref.shape[0]
    experts = slots // capacity
    expert = lax.broadcasted_iota(jnp.int32, (experts, rows), 0)
    earlier = lax.broadcasted_iota(jnp.int32, (rows, rows), 0) < lax.broadcasted_iota(
        jnp.int32, (rows, rows), 1
    )
    earlier = earlier.astype(bf16)
    for copy in copies[:-2]:
        copy.wait()
    copies_out[...] = jnp.broadcast_to(query_ref[...], copies_out.shape)
    tokens = chosen_ref.shape[1] // 2
    here = lax.axis_index("head")
    there = here + 1 - 2 * (here % 2)
    place = lax.broadcasted_iota(jnp.int32, (1, 2 * tokens), 1) // BLK
    blocks = tokens // BLK
    block_of = place + jnp.where(place < blocks, here * blocks, (there - 1) * blocks)
    count = picks_ref.shape[1]
    diagonal = lax.broadcasted_iota(jnp.int32, (count, count), 0) == lax.broadcasted_iota(
        jnp.int32, (count, count), 1
    )
    picks = jnp.sum(jnp.where(diagonal, picks_ref[...], 0), axis=1, keepdims=True)
    chosen = jnp.max((block_of == picks).astype(f32), axis=0, keepdims=True)
    chosen_ref[...] = jnp.broadcast_to(chosen, chosen_ref.shape)
    ids = ids_ref[...]
    picked = jnp.zeros((experts, rows), f32)
    for k in range(top):
        picked = picked + (ids[k : k + 1, :] == expert).astype(f32)
    before = jnp.dot(picked.astype(bf16), earlier, preferred_element_type=f32)
    held = jnp.where(picked > 0.5, before, -1.0)
    slot = lax.broadcasted_iota(jnp.int32, (experts, capacity, rows), 1).astype(f32)
    dispatch = (held[:, None, :] == slot).astype(f32).reshape(slots, rows)
    dispatch_ref[...] = dispatch.astype(bf16)
    combine_ref[...] = dispatch.T.astype(bf16)
    here = lax.axis_index("expert")
    weight = jnp.sum(jnp.where(ids == here, gw_ref[...], 0.0), axis=0, keepdims=True)
    mine = jnp.sum(jnp.where(expert == here, held, 0.0), axis=0, keepdims=True)
    slot = lax.broadcasted_iota(jnp.int32, (capacity, rows), 0).astype(f32)
    weight = jnp.sum(jnp.where(mine == slot, weight, 0.0), axis=1, keepdims=True)
    weight_ref[...] = jnp.broadcast_to(weight, weight_ref.shape)
    width = residual_ref.shape[1]
    residual_out[...] = jnp.concatenate(
        [residual_ref[...].astype(f32), jnp.zeros((rows, LANES - width), f32)], axis=1
    )
    gain = jnp.concatenate(
        [gain_ref[...].astype(f32), jnp.zeros((1, LANES - width), f32)], axis=1
    )
    gain_out[...] = jnp.broadcast_to(gain, gain_out.shape)
    for copy in copies[-2:]:
        copy.wait()
    o_out[...] = o_ref[...]


def values_body(parts_ref, uv_ref, out_ref):
    parts = parts_ref[...].astype(f32)
    heads = parts.shape[1]
    stats = parts[:, :, LAT:]
    scale = stats[:, :, 0:1] + stats[:, :, 1:2]
    total = stats[:, :, 2:3] + stats[:, :, 3:4]
    factor = jnp.exp(scale - jnp.max(scale, axis=0, keepdims=True))
    denominator = jnp.sum(factor * total, axis=0)
    attended = jnp.sum(factor * parts[:, :, :LAT], axis=0) / denominator
    row = lax.broadcasted_iota(jnp.int32, attended.shape, 0)
    spread = jnp.concatenate(
        [jnp.where(row == j, attended, 0.0).astype(bf16) for j in range(heads)], axis=1
    )
    head_vals = jnp.dot(spread, uv_ref[...], preferred_element_type=f32).astype(bf16)
    out_ref[...] = jnp.broadcast_to(head_vals[None], out_ref.shape)


def project_body(vals_ref, o_ref, out_ref):
    order = ring("expert", vals_ref.shape[0])
    vals = jnp.stack([vals_ref[order.index(i)] for i in range(len(order))]).astype(f32)
    wide = jnp.concatenate([vals[:, j, :] for j in range(vals.shape[1])], axis=1).astype(bf16)
    part = lax.dot_general(
        wide, o_ref[...], (((1,), (1,)), ((), ())), preferred_element_type=f32
    ).astype(bf16)
    part = jnp.concatenate(
        [part, jnp.zeros((part.shape[0], LANES - part.shape[1]), bf16)], axis=1
    )
    out_ref[...] = jnp.broadcast_to(part[None], out_ref.shape)


def mix_body(width, parts_ref, residual_ref, gain_ref, dispatch_ref, out_ref, mixed_ref):
    attn = jnp.sum(parts_ref[...].astype(f32), axis=0)
    mixed = (residual_ref[...] + attn).astype(bf16).astype(f32)
    mixed_ref[...] = mixed
    squares = jnp.sum(mixed * mixed, axis=1, keepdims=True)
    top = squares.astype(bf16).astype(f32)
    lane = lax.broadcasted_iota(jnp.int32, mixed.shape, 1)
    scaled = jnp.where(
        lane == width, top, jnp.where(lane == width + 1, squares - top, mixed * gain_ref[0:1])
    )
    slots = jnp.dot(dispatch_ref[...], scaled.astype(bf16), preferred_element_type=f32)
    slots = slots.astype(bf16).reshape(out_ref.shape)
    for i, expert in enumerate(ring("expert", out_ref.shape[0])):
        out_ref[i] = slots[expert]


def expert_body(slots_ref, gate_ref, up_ref, down_ref, weight_ref, out_ref):
    owners, capacity = slots_ref.shape[:2]
    features, units = gate_ref.shape
    width = features // owners
    lane = lax.broadcasted_iota(jnp.int32, (capacity, LANES), 1)
    stats = jnp.sum(slots_ref[...].astype(f32), axis=0)
    stats = jnp.where((lane == width) | (lane == width + 1), stats, 0.0)
    scale = lax.rsqrt(jnp.sum(stats, axis=1, keepdims=True) / features + norm_eps)
    order = ring("expert", owners)
    wide = jnp.concatenate(
        [slots_ref[order.index(i)][:, :width] for i in range(owners)], axis=1
    )
    gate_act = jnp.dot(wide, gate_ref[...], preferred_element_type=f32) * scale
    up_act = jnp.dot(wide, up_ref[...], preferred_element_type=f32) * scale
    hidden = (gate_act / (1.0 + jnp.exp(-gate_act)) * up_act).astype(bf16)
    outcome = jnp.dot(hidden, down_ref[...], preferred_element_type=f32) * weight_ref[:, 0:1]
    pad = jnp.zeros((capacity, LANES - width), f32)
    for i, owner in enumerate(order):
        out_ref[i] = jnp.concatenate(
            [outcome[:, owner * width : (owner + 1) * width], pad], axis=1
        ).astype(bf16)


def gather_body(parts_ref, combine_ref, mixed_ref, out_ref):
    order = ring("expert", parts_ref.shape[0])
    parts = jnp.stack([parts_ref[order.index(i)] for i in range(len(order))])
    parts = parts.reshape(combine_ref.shape[1], LANES)
    share = jnp.dot(combine_ref[...], parts, preferred_element_type=f32)
    share = share + jnp.where(lax.axis_index("head") == 0, mixed_ref[...], 0.0)
    groups, rows = out_ref.shape[0], share.shape[0]
    for i, owner in enumerate(ring("head", groups)):
        group = owner * rows // groups // 8
        out_ref[i] = share[group * 8 : group * 8 + 8]


def finish_body(parts_ref, out_ref):
    share = jnp.sum(parts_ref[...], axis=0)
    rows, columns = out_ref.shape
    place = lax.axis_index("head") % (8 // rows)
    mine = share[:rows]
    for i in range(1, 8 // rows):
        mine = jnp.where(place == i, share[i * rows : (i + 1) * rows], mine)
    out_ref[...] = mine[:, :columns].astype(bf16)


def local(
    queries,
    kv_cache,
    block_ids,
    w_uv,
    o_proj,
    residual,
    moe_gain,
    w_gate,
    w_up,
    w_down,
    expert_ids,
    gate_weights,
):
    head_n = lax.axis_size("head")
    expert_n = lax.axis_size("expert")
    heads, width = queries.shape[1:]
    rows, top = expert_ids.shape
    columns = o_proj.shape[1]
    row_share = rows // head_n
    capacity = min(2 * (rows // expert_n) * top, rows)
    slots = expert_n * capacity

    tokens = kv_cache.shape[1]
    chips = head_n // 2
    alike = [[(head_n // 2 + 2 * i + core) % head_n for i in range(chips)] for core in (0, 1)]
    other = lax.ppermute(kv_cache[0].T, "head", [(i, i ^ 1) for i in range(head_n)])
    staged = pl.pallas_call(
        stage_body,
        out_shape=(
            shape((chips, heads, width), bf16),
            shape((slots, rows), bf16),
            shape((rows, slots), bf16),
            shape((capacity, LANES), f32),
            shape((rows, LANES), f32),
            shape((8, LANES), f32),
            shape((8, 2 * tokens), f32),
            shape(o_proj.shape[::-1], bf16),
            shape((width, tokens), bf16),
        ),
        in_specs=[pl.BlockSpec(memory_space=pltpu.HBM)] * 8,
        out_specs=(VM,) * 9,
        scratch_shapes=[
            pltpu.VMEM(queries.shape, bf16),
            pltpu.VMEM((top, rows), jnp.int32),
            pltpu.VMEM((top, rows), f32),
            pltpu.VMEM((rows, columns), bf16),
            pltpu.VMEM((1, columns), bf16),
            pltpu.VMEM(block_ids.shape, jnp.int32),
            pltpu.VMEM((columns, o_proj.shape[0]), bf16),
            pltpu.SemaphoreType.DMA((8,)),
        ],
        compiler_params=pltpu.CompilerParams(vmem_limit_bytes=48 * 1024 * 1024),
    )(
        *(
            pltpu.with_memory_space_constraint(array, pltpu.HBM)
            for array in (
                queries,
                expert_ids.T,
                gate_weights.T,
                residual,
                moe_gain[None, :],
                block_ids,
                o_proj.T,
                kv_cache[0].T,
            )
        )
    )
    asked, dispatch, combine, weight, residual_wide, gain, chosen, o_proj, cache = staged
    asked = exchange(asked, "head", alike)
    shares = call(
        attend_body,
        shape((chips * heads, LAT + LANES), bf16),
        [VM] * 4,
        chosen,
        asked.reshape(chips * heads, width),
        cache,
        other,
    )
    shares = exchange(shares.reshape(chips, heads, LAT + LANES), "head", alike)
    vals = call(
        values_body,
        shape((expert_n, heads, w_uv.shape[2]), bf16),
        [VM, VM],
        shares,
        w_uv.reshape(heads * LAT, -1),
    )
    vals = exchange(vals, "expert")
    attn = call(project_body, shape((head_n, rows, LANES), bf16), [VM, VM], vals, o_proj)
    attn = exchange(attn, "head")
    tokens, mixed = call(
        functools.partial(mix_body, columns),
        (shape((expert_n, capacity, LANES), bf16), shape((rows, LANES), f32)),
        [VM] * 4,
        attn,
        residual_wide,
        gain,
        dispatch,
    )
    tokens = exchange(tokens, "expert")
    outcome = call(
        expert_body,
        shape((expert_n, capacity, LANES), bf16),
        [VM] * 5,
        tokens,
        w_gate[0],
        w_up[0],
        w_down[0],
        weight,
    )
    outcome = exchange(outcome, "expert")
    moe = call(gather_body, shape((head_n, 8, LANES), f32), [VM] * 3, outcome, combine, mixed)
    return call(finish_body, shape((row_share, columns), bf16), [VM], exchange(moe, "head"))


def solution(mesh):
    in_specs = (
        P("expert", "head", None),
        P("expert", "head", None),
        P("expert", None),
        P("head", None, None),
        P("head", "expert"),
        P(None, "expert"),
        P("expert"),
        P("expert", None, "head"),
        P("expert", None, "head"),
        P("expert", "head", None),
        P(),
        P(),
    )
    out_specs = P("head", "expert")
    return jax.shard_map(local, mesh=mesh, in_specs=in_specs, out_specs=out_specs, check_vma=False)
```

```python
import functools

import jax
import jax.numpy as jnp
from jax import lax
from jax.experimental import pallas as pl
from jax.experimental.pallas import tpu as pltpu
from jax.sharding import PartitionSpec as P

LAT = 512
BLK = 64
LANES = 128
NEG = -1e30

score_scale = 192 ** (-0.5)
norm_eps = 1e-06

f32 = jnp.float32
bf16 = jnp.bfloat16


VM = pl.BlockSpec(memory_space=pltpu.VMEM)
SM = pl.BlockSpec(memory_space=pltpu.SMEM)
shape = jax.ShapeDtypeStruct


def call(body, out_shape, in_specs, *operands):
    return pl.pallas_call(
        body,
        out_shape=out_shape,
        in_specs=in_specs,
        out_specs=jax.tree.map(lambda _: VM, out_shape),
        compiler_params=pltpu.CompilerParams(vmem_limit_bytes=48 * 1024 * 1024),
    )(*operands)


def ring(axis, count):
    first = count // 2 + 3 if axis == "head" else count * 11 // 16
    return [(first + i) % count for i in range(count)]


def exchange(blocks, axis, groups=None):
    groups = groups or [ring(axis, blocks.shape[0])]
    return lax.all_to_all(
        blocks, axis, split_axis=0, concat_axis=0, tiled=True, axis_index_groups=groups
    )


def attend_body(chosen_ref, q_ref, mine_ref, other_ref, out_ref):
    caches = (mine_ref, other_ref)
    chosen = chosen_ref[0:1] > 0.5
    scores = jnp.concatenate(
        [jnp.dot(q_ref[...], ref[...], preferred_element_type=f32) for ref in caches], axis=1
    )
    scores = jnp.where(chosen, scores * score_scale, NEG)
    highest = jnp.max(scores, axis=1, keepdims=True)
    top = highest.astype(bf16).astype(f32)
    rest = (highest - top).astype(bf16).astype(f32)
    weights = jnp.where(chosen, jnp.exp(scores - (top + rest)), 0.0)
    total = jnp.sum(weights, axis=1, keepdims=True)
    weights = weights.astype(bf16)
    tokens = mine_ref.shape[1]
    latent = sum(
        lax.dot_general(
            weights[:, i * tokens : (i + 1) * tokens],
            ref[:LAT, :],
            (((1,), (1,)), ((), ())),
            preferred_element_type=f32,
        )
        for i, ref in enumerate(caches)
    )
    total_top = total.astype(bf16).astype(f32)
    total_rest = total - total_top
    lane = lax.broadcasted_iota(jnp.int32, (q_ref.shape[0], LANES), 1)
    stats = jnp.where(
        lane == 0, top, jnp.where(lane == 1, rest, jnp.where(lane == 2, total_top, total_rest))
    )
    out_ref[:, :LAT] = latent.astype(bf16)
    out_ref[:, LAT:] = stats.astype(bf16)


def stage_body(
    queries_any, ids_any, gw_any, residual_any, gain_any, picks_any, o_any, cache_any,
    copies_out, dispatch_ref, combine_ref, weight_ref, residual_out, gain_out, chosen_ref, o_out, cache_out,
    query_ref, ids_ref, gw_ref, residual_ref, gain_ref, picks_ref, o_ref, sems,
):
    pairs = (
        (queries_any, query_ref),
        (ids_any, ids_ref),
        (gw_any, gw_ref),
        (residual_any, residual_ref),
        (gain_any, gain_ref),
        (picks_any, picks_ref),
        (o_any, o_ref),
        (cache_any, cache_out),
    )
    copies = [pltpu.make_async_copy(a, b, sems.at[i]) for i, (a, b) in enumerate(pairs)]
    for copy in copies:
        copy.start()
    top, rows = ids_ref.shape
    slots = combine_ref.shape[1]
    capacity = weight_ref.shape[0]
    experts = slots // capacity
    expert = lax.broadcasted_iota(jnp.int32, (experts, rows), 0)
    earlier = lax.broadcasted_iota(jnp.int32, (rows, rows), 0) < lax.broadcasted_iota(
        jnp.int32, (rows, rows), 1
    )
    earlier = earlier.astype(bf16)
    for copy in copies[:-2]:
        copy.wait()
    copies_out[...] = jnp.broadcast_to(query_ref[...], copies_out.shape)
    tokens = chosen_ref.shape[1] // 2
    here = lax.axis_index("head")
    there = here + 1 - 2 * (here % 2)
    place = lax.broadcasted_iota(jnp.int32, (1, 2 * tokens), 1) // BLK
    blocks = tokens // BLK
    block_of = place + jnp.where(place < blocks, here * blocks, (there - 1) * blocks)
    count = picks_ref.shape[1]
    diagonal = lax.broadcasted_iota(jnp.int32, (count, count), 0) == lax.broadcasted_iota(
        jnp.int32, (count, count), 1
    )
    picks = jnp.sum(jnp.where(diagonal, picks_ref[...], 0), axis=1, keepdims=True)
    chosen = jnp.max((block_of == picks).astype(f32), axis=0, keepdims=True)
    chosen_ref[...] = jnp.broadcast_to(chosen, chosen_ref.shape)
    ids = ids_ref[...]
    picked = jnp.zeros((experts, rows), f32)
    for k in range(top):
        picked = picked + (ids[k : k + 1, :] == expert).astype(f32)
    before = jnp.dot(picked.astype(bf16), earlier, preferred_element_type=f32)
    held = jnp.where(picked > 0.5, before, -1.0)
    slot = lax.broadcasted_iota(jnp.int32, (experts, capacity, rows), 1).astype(f32)
    dispatch = (held[:, None, :] == slot).astype(f32).reshape(slots, rows)
    dispatch_ref[...] = dispatch.astype(bf16)
    combine_ref[...] = dispatch.T.astype(bf16)
    here = lax.axis_index("expert")
    weight = jnp.sum(jnp.where(ids == here, gw_ref[...], 0.0), axis=0, keepdims=True)
    mine = jnp.sum(jnp.where(expert == here, held, 0.0), axis=0, keepdims=True)
    slot = lax.broadcasted_iota(jnp.int32, (capacity, rows), 0).astype(f32)
    weight = jnp.sum(jnp.where(mine == slot, weight, 0.0), axis=1, keepdims=True)
    weight_ref[...] = jnp.broadcast_to(weight, weight_ref.shape)
    width = residual_ref.shape[1]
    residual_out[...] = jnp.concatenate(
        [residual_ref[...].astype(f32), jnp.zeros((rows, LANES - width), f32)], axis=1
    )
    gain = jnp.concatenate(
        [gain_ref[...].astype(f32), jnp.zeros((1, LANES - width), f32)], axis=1
    )
    gain_out[...] = jnp.broadcast_to(gain, gain_out.shape)
    for copy in copies[-2:]:
        copy.wait()
    o_out[...] = o_ref[...]


def values_body(parts_ref, uv_ref, out_ref):
    parts = parts_ref[...].astype(f32)
    heads = parts.shape[1]
    stats = parts[:, :, LAT:]
    scale = stats[:, :, 0:1] + stats[:, :, 1:2]
    total = stats[:, :, 2:3] + stats[:, :, 3:4]
    factor = jnp.exp(scale - jnp.max(scale, axis=0, keepdims=True))
    denominator = jnp.sum(factor * total, axis=0)
    attended = jnp.sum(factor * parts[:, :, :LAT], axis=0) / denominator
    row = lax.broadcasted_iota(jnp.int32, attended.shape, 0)
    spread = jnp.concatenate(
        [jnp.where(row == j, attended, 0.0).astype(bf16) for j in range(heads)], axis=1
    )
    head_vals = jnp.dot(spread, uv_ref[...], preferred_element_type=f32).astype(bf16)
    out_ref[...] = jnp.broadcast_to(head_vals[None], out_ref.shape)


def project_body(vals_ref, o_ref, out_ref):
    order = ring("expert", vals_ref.shape[0])
    vals = jnp.stack([vals_ref[order.index(i)] for i in range(len(order))]).astype(f32)
    wide = jnp.concatenate([vals[:, j, :] for j in range(vals.shape[1])], axis=1).astype(bf16)
    part = lax.dot_general(
        wide, o_ref[...], (((1,), (1,)), ((), ())), preferred_element_type=f32
    ).astype(bf16)
    part = jnp.concatenate(
        [part, jnp.zeros((part.shape[0], LANES - part.shape[1]), bf16)], axis=1
    )
    out_ref[...] = jnp.broadcast_to(part[None], out_ref.shape)


def mix_body(width, parts_ref, residual_ref, gain_ref, dispatch_ref, out_ref, mixed_ref):
    attn = jnp.sum(parts_ref[...].astype(f32), axis=0)
    mixed = (residual_ref[...] + attn).astype(bf16).astype(f32)
    mixed_ref[...] = mixed
    squares = jnp.sum(mixed * mixed, axis=1, keepdims=True)
    top = squares.astype(bf16).astype(f32)
    lane = lax.broadcasted_iota(jnp.int32, mixed.shape, 1)
    scaled = jnp.where(
        lane == width, top, jnp.where(lane == width + 1, squares - top, mixed * gain_ref[0:1])
    )
    slots = jnp.dot(dispatch_ref[...], scaled.astype(bf16), preferred_element_type=f32)
    slots = slots.astype(bf16).reshape(out_ref.shape)
    for i, expert in enumerate(ring("expert", out_ref.shape[0])):
        out_ref[i] = slots[expert]


def expert_body(slots_ref, gate_ref, up_ref, down_ref, weight_ref, out_ref):
    owners, capacity = slots_ref.shape[:2]
    features, units = gate_ref.shape
    width = features // owners
    lane = lax.broadcasted_iota(jnp.int32, (capacity, LANES), 1)
    stats = jnp.sum(slots_ref[...].astype(f32), axis=0)
    stats = jnp.where((lane == width) | (lane == width + 1), stats, 0.0)
    scale = lax.rsqrt(jnp.sum(stats, axis=1, keepdims=True) / features + norm_eps)
    order = ring("expert", owners)
    wide = jnp.concatenate(
        [slots_ref[order.index(i)][:, :width] for i in range(owners)], axis=1
    )
    gate_act = jnp.dot(wide, gate_ref[...], preferred_element_type=f32) * scale
    up_act = jnp.dot(wide, up_ref[...], preferred_element_type=f32) * scale
    hidden = (gate_act / (1.0 + jnp.exp(-gate_act)) * up_act).astype(bf16)
    outcome = jnp.dot(hidden, down_ref[...], preferred_element_type=f32) * weight_ref[:, 0:1]
    pad = jnp.zeros((capacity, LANES - width), f32)
    for i, owner in enumerate(order):
        out_ref[i] = jnp.concatenate(
            [outcome[:, owner * width : (owner + 1) * width], pad], axis=1
        ).astype(bf16)


def gather_body(parts_ref, combine_ref, mixed_ref, out_ref):
    order = ring("expert", parts_ref.shape[0])
    parts = jnp.stack([parts_ref[order.index(i)] for i in range(len(order))])
    parts = parts.reshape(combine_ref.shape[1], LANES)
    share = jnp.dot(combine_ref[...], parts, preferred_element_type=f32)
    share = share + jnp.where(lax.axis_index("head") == 0, mixed_ref[...], 0.0)
    groups, rows = out_ref.shape[0], share.shape[0]
    for i, owner in enumerate(ring("head", groups)):
        group = owner * rows // groups // 8
        out_ref[i] = share[group * 8 : group * 8 + 8]


def finish_body(parts_ref, out_ref):
    share = jnp.sum(parts_ref[...], axis=0)
    rows, columns = out_ref.shape
    place = lax.axis_index("head") % (8 // rows)
    mine = share[:rows]
    for i in range(1, 8 // rows):
        mine = jnp.where(place == i, share[i * rows : (i + 1) * rows], mine)
    out_ref[...] = mine[:, :columns].astype(bf16)


def local(
    queries,
    kv_cache,
    block_ids,
    w_uv,
    o_proj,
    residual,
    moe_gain,
    w_gate,
    w_up,
    w_down,
    expert_ids,
    gate_weights,
):
    head_n = lax.axis_size("head")
    expert_n = lax.axis_size("expert")
    heads, width = queries.shape[1:]
    rows, top = expert_ids.shape
    columns = o_proj.shape[1]
    row_share = rows // head_n
    capacity = min(2 * (rows // expert_n) * top, rows)
    slots = expert_n * capacity

    tokens = kv_cache.shape[1]
    chips = head_n // 2
    alike = [[(head_n // 2 + 2 + 2 * i + core) % head_n for i in range(chips)] for core in (0, 1)]
    other = lax.ppermute(kv_cache[0].T, "head", [(i, i ^ 1) for i in range(head_n)])
    staged = pl.pallas_call(
        stage_body,
        out_shape=(
            shape((chips, heads, width), bf16),
            shape((slots, rows), bf16),
            shape((rows, slots), bf16),
            shape((capacity, LANES), f32),
            shape((rows, LANES), f32),
            shape((8, LANES), f32),
            shape((8, 2 * tokens), f32),
            shape(o_proj.shape[::-1], bf16),
            shape((width, tokens), bf16),
        ),
        in_specs=[pl.BlockSpec(memory_space=pltpu.HBM)] * 8,
        out_specs=(VM,) * 9,
        scratch_shapes=[
            pltpu.VMEM(queries.shape, bf16),
            pltpu.VMEM((top, rows), jnp.int32),
            pltpu.VMEM((top, rows), f32),
            pltpu.VMEM((rows, columns), bf16),
            pltpu.VMEM((1, columns), bf16),
            pltpu.VMEM(block_ids.shape, jnp.int32),
            pltpu.VMEM((columns, o_proj.shape[0]), bf16),
            pltpu.SemaphoreType.DMA((8,)),
        ],
        compiler_params=pltpu.CompilerParams(vmem_limit_bytes=48 * 1024 * 1024),
    )(
        *(
            pltpu.with_memory_space_constraint(array, pltpu.HBM)
            for array in (
                queries,
                expert_ids.T,
                gate_weights.T,
                residual,
                moe_gain[None, :],
                block_ids,
                o_proj.T,
                kv_cache[0].T,
            )
        )
    )
    asked, dispatch, combine, weight, residual_wide, gain, chosen, o_proj, cache = staged
    asked = exchange(asked, "head", alike)
    shares = call(
        attend_body,
        shape((chips * heads, LAT + LANES), bf16),
        [VM] * 4,
        chosen,
        asked.reshape(chips * heads, width),
        cache,
        other,
    )
    shares = exchange(shares.reshape(chips, heads, LAT + LANES), "head", alike)
    vals = call(
        values_body,
        shape((expert_n, heads, w_uv.shape[2]), bf16),
        [VM, VM],
        shares,
        w_uv.reshape(heads * LAT, -1),
    )
    vals = exchange(vals, "expert")
    attn = call(project_body, shape((head_n, rows, LANES), bf16), [VM, VM], vals, o_proj)
    attn = exchange(attn, "head")
    tokens, mixed = call(
        functools.partial(mix_body, columns),
        (shape((expert_n, capacity, LANES), bf16), shape((rows, LANES), f32)),
        [VM] * 4,
        attn,
        residual_wide,
        gain,
        dispatch,
    )
    tokens = exchange(tokens, "expert")
    outcome = call(
        expert_body,
        shape((expert_n, capacity, LANES), bf16),
        [VM] * 5,
        tokens,
        w_gate[0],
        w_up[0],
        w_down[0],
        weight,
    )
    outcome = exchange(outcome, "expert")
    moe = call(gather_body, shape((head_n, 8, LANES), f32), [VM] * 3, outcome, combine, mixed)
    return call(finish_body, shape((row_share, columns), bf16), [VM], exchange(moe, "head"))


def solution(mesh):
    in_specs = (
        P("expert", "head", None),
        P("expert", "head", None),
        P("expert", None),
        P("head", None, None),
        P("head", "expert"),
        P(None, "expert"),
        P("expert"),
        P("expert", None, "head"),
        P("expert", None, "head"),
        P("expert", "head", None),
        P(),
        P(),
    )
    out_specs = P("head", "expert")
    return jax.shard_map(local, mesh=mesh, in_specs=in_specs, out_specs=out_specs, check_vma=False)
```

```python
import functools

import jax
import jax.numpy as jnp
from jax import lax
from jax.experimental import pallas as pl
from jax.experimental.pallas import tpu as pltpu
from jax.sharding import PartitionSpec as P

LAT = 512
BLK = 64
LANES = 128
NEG = -1e30

score_scale = 192 ** (-0.5)
norm_eps = 1e-06

f32 = jnp.float32
bf16 = jnp.bfloat16


VM = pl.BlockSpec(memory_space=pltpu.VMEM)
SM = pl.BlockSpec(memory_space=pltpu.SMEM)
shape = jax.ShapeDtypeStruct


def call(body, out_shape, in_specs, *operands):
    return pl.pallas_call(
        body,
        out_shape=out_shape,
        in_specs=in_specs,
        out_specs=jax.tree.map(lambda _: VM, out_shape),
        compiler_params=pltpu.CompilerParams(vmem_limit_bytes=48 * 1024 * 1024),
    )(*operands)


def ring(axis, count):
    first = count // 2 + 3 if axis == "head" else count * 11 // 16
    return [(first + i) % count for i in range(count)]


def exchange(blocks, axis, groups=None):
    groups = groups or [ring(axis, blocks.shape[0])]
    return lax.all_to_all(
        blocks, axis, split_axis=0, concat_axis=0, tiled=True, axis_index_groups=groups
    )


def attend_body(chosen_ref, q_ref, mine_ref, other_ref, out_ref):
    caches = (mine_ref, other_ref)
    chosen = chosen_ref[0:1] > 0.5
    scores = jnp.concatenate(
        [jnp.dot(q_ref[...], ref[...], preferred_element_type=f32) for ref in caches], axis=1
    )
    scores = jnp.where(chosen, scores * score_scale, NEG)
    highest = jnp.max(scores, axis=1, keepdims=True)
    top = highest.astype(bf16).astype(f32)
    rest = (highest - top).astype(bf16).astype(f32)
    weights = jnp.where(chosen, jnp.exp(scores - (top + rest)), 0.0)
    total = jnp.sum(weights, axis=1, keepdims=True)
    weights = weights.astype(bf16)
    tokens = mine_ref.shape[1]
    latent = sum(
        lax.dot_general(
            weights[:, i * tokens : (i + 1) * tokens],
            ref[:LAT, :],
            (((1,), (1,)), ((), ())),
            preferred_element_type=f32,
        )
        for i, ref in enumerate(caches)
    )
    total_top = total.astype(bf16).astype(f32)
    total_rest = total - total_top
    lane = lax.broadcasted_iota(jnp.int32, (q_ref.shape[0], LANES), 1)
    stats = jnp.where(
        lane == 0, top, jnp.where(lane == 1, rest, jnp.where(lane == 2, total_top, total_rest))
    )
    out_ref[:, :LAT] = latent.astype(bf16)
    out_ref[:, LAT:] = stats.astype(bf16)


def stage_body(
    queries_any, ids_any, gw_any, residual_any, gain_any, picks_any, o_any, cache_any,
    copies_out, dispatch_ref, combine_ref, weight_ref, residual_out, gain_out, chosen_ref, o_out, cache_out,
    ids_ref, gw_ref, residual_ref, gain_ref, picks_ref, sems,
):
    pairs = (
        (queries_any, copies_out.at[pl.ds(0, 1)]),
        (ids_any, ids_ref),
        (gw_any, gw_ref),
        (residual_any, residual_ref),
        (gain_any, gain_ref),
        (picks_any, picks_ref),
        (o_any, o_out),
        (cache_any, cache_out),
    )
    copies = [pltpu.make_async_copy(a, b, sems.at[i]) for i, (a, b) in enumerate(pairs)]
    for copy in copies:
        copy.start()
    top, rows = ids_ref.shape
    slots = combine_ref.shape[1]
    capacity = weight_ref.shape[0]
    experts = slots // capacity
    expert = lax.broadcasted_iota(jnp.int32, (experts, rows), 0)
    earlier = lax.broadcasted_iota(jnp.int32, (rows, rows), 0) < lax.broadcasted_iota(
        jnp.int32, (rows, rows), 1
    )
    earlier = earlier.astype(bf16)
    for copy in copies[:-2]:
        copy.wait()
    others = copies_out.shape[0] - 1
    copies_out[1:] = jnp.broadcast_to(copies_out[0:1], (others,) + copies_out.shape[1:])
    tokens = chosen_ref.shape[1] // 2
    here = lax.axis_index("head")
    there = here + 1 - 2 * (here % 2)
    place = lax.broadcasted_iota(jnp.int32, (1, 2 * tokens), 1) // BLK
    blocks = tokens // BLK
    block_of = place + jnp.where(place < blocks, here * blocks, (there - 1) * blocks)
    count = picks_ref.shape[1]
    diagonal = lax.broadcasted_iota(jnp.int32, (count, count), 0) == lax.broadcasted_iota(
        jnp.int32, (count, count), 1
    )
    picks = jnp.sum(jnp.where(diagonal, picks_ref[...], 0), axis=1, keepdims=True)
    chosen = jnp.max((block_of == picks).astype(f32), axis=0, keepdims=True)
    chosen_ref[...] = jnp.broadcast_to(chosen, chosen_ref.shape)
    ids = ids_ref[...]
    picked = jnp.zeros((experts, rows), f32)
    for k in range(top):
        picked = picked + (ids[k : k + 1, :] == expert).astype(f32)
    before = jnp.dot(picked.astype(bf16), earlier, preferred_element_type=f32)
    held = jnp.where(picked > 0.5, before, -1.0)
    slot = lax.broadcasted_iota(jnp.int32, (experts, capacity, rows), 1).astype(f32)
    dispatch = (held[:, None, :] == slot).astype(f32).reshape(slots, rows)
    dispatch_ref[...] = dispatch.astype(bf16)
    combine_ref[...] = dispatch.T.astype(bf16)
    here = lax.axis_index("expert")
    weight = jnp.sum(jnp.where(ids == here, gw_ref[...], 0.0), axis=0, keepdims=True)
    mine = jnp.sum(jnp.where(expert == here, held, 0.0), axis=0, keepdims=True)
    slot = lax.broadcasted_iota(jnp.int32, (capacity, rows), 0).astype(f32)
    weight = jnp.sum(jnp.where(mine == slot, weight, 0.0), axis=1, keepdims=True)
    weight_ref[...] = jnp.broadcast_to(weight, weight_ref.shape)
    width = residual_ref.shape[1]
    residual_out[...] = jnp.concatenate(
        [residual_ref[...].astype(f32), jnp.zeros((rows, LANES - width), f32)], axis=1
    )
    gain = jnp.concatenate(
        [gain_ref[...].astype(f32), jnp.zeros((1, LANES - width), f32)], axis=1
    )
    gain_out[...] = jnp.broadcast_to(gain, gain_out.shape)
    for copy in copies[-2:]:
        copy.wait()


def values_body(parts_ref, uv_ref, out_ref):
    parts = parts_ref[...].astype(f32)
    heads = parts.shape[1]
    stats = parts[:, :, LAT:]
    scale = stats[:, :, 0:1] + stats[:, :, 1:2]
    total = stats[:, :, 2:3] + stats[:, :, 3:4]
    factor = jnp.exp(scale - jnp.max(scale, axis=0, keepdims=True))
    denominator = jnp.sum(factor * total, axis=0)
    attended = jnp.sum(factor * parts[:, :, :LAT], axis=0) / denominator
    row = lax.broadcasted_iota(jnp.int32, attended.shape, 0)
    spread = jnp.concatenate(
        [jnp.where(row == j, attended, 0.0).astype(bf16) for j in range(heads)], axis=1
    )
    head_vals = jnp.dot(spread, uv_ref[...], preferred_element_type=f32).astype(bf16)
    out_ref[...] = jnp.broadcast_to(head_vals[None], out_ref.shape)


def project_body(vals_ref, o_ref, out_ref):
    order = ring("expert", vals_ref.shape[0])
    vals = jnp.stack([vals_ref[order.index(i)] for i in range(len(order))]).astype(f32)
    wide = jnp.concatenate([vals[:, j, :] for j in range(vals.shape[1])], axis=1).astype(bf16)
    part = lax.dot_general(
        wide, o_ref[...], (((1,), (1,)), ((), ())), preferred_element_type=f32
    ).astype(bf16)
    part = jnp.concatenate(
        [part, jnp.zeros((part.shape[0], LANES - part.shape[1]), bf16)], axis=1
    )
    out_ref[...] = jnp.broadcast_to(part[None], out_ref.shape)


def mix_body(width, parts_ref, residual_ref, gain_ref, dispatch_ref, out_ref, mixed_ref):
    attn = jnp.sum(parts_ref[...].astype(f32), axis=0)
    mixed = (residual_ref[...] + attn).astype(bf16).astype(f32)
    mixed_ref[...] = mixed
    squares = jnp.sum(mixed * mixed, axis=1, keepdims=True)
    top = squares.astype(bf16).astype(f32)
    lane = lax.broadcasted_iota(jnp.int32, mixed.shape, 1)
    scaled = jnp.where(
        lane == width, top, jnp.where(lane == width + 1, squares - top, mixed * gain_ref[0:1])
    )
    slots = jnp.dot(dispatch_ref[...], scaled.astype(bf16), preferred_element_type=f32)
    slots = slots.astype(bf16).reshape(out_ref.shape)
    for i, expert in enumerate(ring("expert", out_ref.shape[0])):
        out_ref[i] = slots[expert]


def expert_body(slots_ref, gate_ref, up_ref, down_ref, weight_ref, out_ref):
    owners, capacity = slots_ref.shape[:2]
    features, units = gate_ref.shape
    width = features // owners
    lane = lax.broadcasted_iota(jnp.int32, (capacity, LANES), 1)
    stats = jnp.sum(slots_ref[...].astype(f32), axis=0)
    stats = jnp.where((lane == width) | (lane == width + 1), stats, 0.0)
    scale = lax.rsqrt(jnp.sum(stats, axis=1, keepdims=True) / features + norm_eps)
    order = ring("expert", owners)
    wide = jnp.concatenate(
        [slots_ref[order.index(i)][:, :width] for i in range(owners)], axis=1
    )
    gate_act = jnp.dot(wide, gate_ref[...], preferred_element_type=f32) * scale
    up_act = jnp.dot(wide, up_ref[...], preferred_element_type=f32) * scale
    hidden = (gate_act / (1.0 + jnp.exp(-gate_act)) * up_act).astype(bf16)
    outcome = jnp.dot(hidden, down_ref[...], preferred_element_type=f32) * weight_ref[:, 0:1]
    pad = jnp.zeros((capacity, LANES - width), f32)
    for i, owner in enumerate(order):
        out_ref[i] = jnp.concatenate(
            [outcome[:, owner * width : (owner + 1) * width], pad], axis=1
        ).astype(bf16)


def gather_body(parts_ref, combine_ref, mixed_ref, out_ref):
    order = ring("expert", parts_ref.shape[0])
    parts = jnp.stack([parts_ref[order.index(i)] for i in range(len(order))])
    parts = parts.reshape(combine_ref.shape[1], LANES)
    share = jnp.dot(combine_ref[...], parts, preferred_element_type=f32)
    share = share + jnp.where(lax.axis_index("head") == 0, mixed_ref[...], 0.0)
    groups, rows = out_ref.shape[0], share.shape[0]
    for i, owner in enumerate(ring("head", groups)):
        group = owner * rows // groups // 8
        out_ref[i] = share[group * 8 : group * 8 + 8]


def finish_body(parts_ref, out_ref):
    share = jnp.sum(parts_ref[...], axis=0)
    rows, columns = out_ref.shape
    place = lax.axis_index("head") % (8 // rows)
    mine = share[:rows]
    for i in range(1, 8 // rows):
        mine = jnp.where(place == i, share[i * rows : (i + 1) * rows], mine)
    out_ref[...] = mine[:, :columns].astype(bf16)


def local(
    queries,
    kv_cache,
    block_ids,
    w_uv,
    o_proj,
    residual,
    moe_gain,
    w_gate,
    w_up,
    w_down,
    expert_ids,
    gate_weights,
):
    head_n = lax.axis_size("head")
    expert_n = lax.axis_size("expert")
    heads, width = queries.shape[1:]
    rows, top = expert_ids.shape
    columns = o_proj.shape[1]
    row_share = rows // head_n
    capacity = min(2 * (rows // expert_n) * top, rows)
    slots = expert_n * capacity

    tokens = kv_cache.shape[1]
    chips = head_n // 2
    alike = [[(head_n // 2 + 2 + 2 * i + core) % head_n for i in range(chips)] for core in (0, 1)]
    other = lax.ppermute(kv_cache[0].T, "head", [(i, i ^ 1) for i in range(head_n)])
    staged = pl.pallas_call(
        stage_body,
        out_shape=(
            shape((chips, heads, width), bf16),
            shape((slots, rows), bf16),
            shape((rows, slots), bf16),
            shape((capacity, LANES), f32),
            shape((rows, LANES), f32),
            shape((8, LANES), f32),
            shape((8, 2 * tokens), f32),
            shape(o_proj.shape[::-1], bf16),
            shape((width, tokens), bf16),
        ),
        in_specs=[pl.BlockSpec(memory_space=pltpu.HBM)] * 8,
        out_specs=(VM,) * 9,
        scratch_shapes=[
            pltpu.VMEM((top, rows), jnp.int32),
            pltpu.VMEM((top, rows), f32),
            pltpu.VMEM((rows, columns), bf16),
            pltpu.VMEM((1, columns), bf16),
            pltpu.VMEM(block_ids.shape, jnp.int32),
            pltpu.SemaphoreType.DMA((8,)),
        ],
        compiler_params=pltpu.CompilerParams(vmem_limit_bytes=48 * 1024 * 1024),
    )(
        *(
            pltpu.with_memory_space_constraint(array, pltpu.HBM)
            for array in (
                queries,
                expert_ids.T,
                gate_weights.T,
                residual,
                moe_gain[None, :],
                block_ids,
                o_proj.T,
                kv_cache[0].T,
            )
        )
    )
    asked, dispatch, combine, weight, residual_wide, gain, chosen, o_proj, cache = staged
    asked = exchange(asked, "head", alike)
    shares = call(
        attend_body,
        shape((chips * heads, LAT + LANES), bf16),
        [VM] * 4,
        chosen,
        asked.reshape(chips * heads, width),
        cache,
        other,
    )
    shares = exchange(shares.reshape(chips, heads, LAT + LANES), "head", alike)
    vals = call(
        values_body,
        shape((expert_n, heads, w_uv.shape[2]), bf16),
        [VM, VM],
        shares,
        w_uv.reshape(heads * LAT, -1),
    )
    vals = exchange(vals, "expert")
    attn = call(project_body, shape((head_n, rows, LANES), bf16), [VM, VM], vals, o_proj)
    attn = exchange(attn, "head")
    tokens, mixed = call(
        functools.partial(mix_body, columns),
        (shape((expert_n, capacity, LANES), bf16), shape((rows, LANES), f32)),
        [VM] * 4,
        attn,
        residual_wide,
        gain,
        dispatch,
    )
    tokens = exchange(tokens, "expert")
    outcome = call(
        expert_body,
        shape((expert_n, capacity, LANES), bf16),
        [VM] * 5,
        tokens,
        w_gate[0],
        w_up[0],
        w_down[0],
        weight,
    )
    outcome = exchange(outcome, "expert")
    moe = call(gather_body, shape((head_n, 8, LANES), f32), [VM] * 3, outcome, combine, mixed)
    return call(finish_body, shape((row_share, columns), bf16), [VM], exchange(moe, "head"))


def solution(mesh):
    in_specs = (
        P("expert", "head", None),
        P("expert", "head", None),
        P("expert", None),
        P("head", None, None),
        P("head", "expert"),
        P(None, "expert"),
        P("expert"),
        P("expert", None, "head"),
        P("expert", None, "head"),
        P("expert", "head", None),
        P(),
        P(),
    )
    out_specs = P("head", "expert")
    return jax.shard_map(local, mesh=mesh, in_specs=in_specs, out_specs=out_specs, check_vma=False)
```

```python
import functools

import jax
import jax.numpy as jnp
from jax import lax
from jax.experimental import pallas as pl
from jax.experimental.pallas import tpu as pltpu
from jax.sharding import PartitionSpec as P

LAT = 512
BLK = 64
LANES = 128
NEG = -1e30

score_scale = 192 ** (-0.5)
norm_eps = 1e-06

f32 = jnp.float32
bf16 = jnp.bfloat16


VM = pl.BlockSpec(memory_space=pltpu.VMEM)
SM = pl.BlockSpec(memory_space=pltpu.SMEM)
shape = jax.ShapeDtypeStruct


def call(body, out_shape, in_specs, *operands):
    return pl.pallas_call(
        body,
        out_shape=out_shape,
        in_specs=in_specs,
        out_specs=jax.tree.map(lambda _: VM, out_shape),
        compiler_params=pltpu.CompilerParams(vmem_limit_bytes=48 * 1024 * 1024),
    )(*operands)


def ring(axis, count):
    first = count // 2 + 3 if axis == "head" else count * 11 // 16
    return [(first + i) % count for i in range(count)]


def exchange(blocks, axis, groups=None):
    groups = groups or [ring(axis, blocks.shape[0])]
    return lax.all_to_all(
        blocks, axis, split_axis=0, concat_axis=0, tiled=True, axis_index_groups=groups
    )


def attend_body(chosen_ref, q_ref, mine_ref, other_ref, out_ref):
    caches = (mine_ref, other_ref)
    chosen = chosen_ref[0:1] > 0.5
    scores = jnp.concatenate(
        [jnp.dot(q_ref[...], ref[...], preferred_element_type=f32) for ref in caches], axis=1
    )
    scores = jnp.where(chosen, scores * score_scale, NEG)
    highest = jnp.max(scores, axis=1, keepdims=True)
    top = highest.astype(bf16).astype(f32)
    rest = (highest - top).astype(bf16).astype(f32)
    weights = jnp.where(chosen, jnp.exp(scores - (top + rest)), 0.0)
    total = jnp.sum(weights, axis=1, keepdims=True)
    weights = weights.astype(bf16)
    tokens = mine_ref.shape[1]
    latent = sum(
        lax.dot_general(
            weights[:, i * tokens : (i + 1) * tokens],
            ref[:LAT, :],
            (((1,), (1,)), ((), ())),
            preferred_element_type=f32,
        )
        for i, ref in enumerate(caches)
    )
    total_top = total.astype(bf16).astype(f32)
    total_rest = total - total_top
    lane = lax.broadcasted_iota(jnp.int32, (q_ref.shape[0], LANES), 1)
    stats = jnp.where(
        lane == 0, top, jnp.where(lane == 1, rest, jnp.where(lane == 2, total_top, total_rest))
    )
    out_ref[:, :LAT] = latent.astype(bf16)
    out_ref[:, LAT:] = stats.astype(bf16)


def stage_body(
    queries_any, ids_any, gw_any, residual_any, gain_any, picks_any, o_any, cache_any,
    copies_out, dispatch_ref, combine_ref, weight_ref, residual_out, gain_out, chosen_ref, o_out, cache_out,
    query_ref, ids_ref, gw_ref, residual_ref, gain_ref, picks_ref, o_ref, sems,
):
    pairs = (
        (queries_any, query_ref),
        (ids_any, ids_ref),
        (gw_any, gw_ref),
        (residual_any, residual_ref),
        (gain_any, gain_ref),
        (picks_any, picks_ref),
        (o_any, o_ref),
        (cache_any, cache_out),
    )
    copies = [pltpu.make_async_copy(a, b, sems.at[i]) for i, (a, b) in enumerate(pairs)]
    for copy in copies:
        copy.start()
    top, rows = ids_ref.shape
    slots = combine_ref.shape[1]
    capacity = weight_ref.shape[0]
    experts = slots // capacity
    expert = lax.broadcasted_iota(jnp.int32, (experts, rows), 0)
    earlier = lax.broadcasted_iota(jnp.int32, (rows, rows), 0) < lax.broadcasted_iota(
        jnp.int32, (rows, rows), 1
    )
    earlier = earlier.astype(bf16)
    for copy in copies[:-2]:
        copy.wait()
    copies_out[...] = jnp.broadcast_to(query_ref[...], copies_out.shape)
    tokens = chosen_ref.shape[1] // 2
    here = lax.axis_index("head")
    there = here + 1 - 2 * (here % 2)
    place = lax.broadcasted_iota(jnp.int32, (1, 2 * tokens), 1) // BLK
    blocks = tokens // BLK
    block_of = place + jnp.where(place < blocks, here * blocks, (there - 1) * blocks)
    count = picks_ref.shape[1]
    diagonal = lax.broadcasted_iota(jnp.int32, (count, count), 0) == lax.broadcasted_iota(
        jnp.int32, (count, count), 1
    )
    picks = jnp.sum(jnp.where(diagonal, picks_ref[...], 0), axis=1, keepdims=True)
    chosen = jnp.max((block_of == picks).astype(f32), axis=0, keepdims=True)
    chosen_ref[...] = jnp.broadcast_to(chosen, chosen_ref.shape)
    ids = ids_ref[...]
    picked = jnp.zeros((experts, rows), f32)
    for k in range(top):
        picked = picked + (ids[k : k + 1, :] == expert).astype(f32)
    before = jnp.dot(picked.astype(bf16), earlier, preferred_element_type=f32)
    held = jnp.where(picked > 0.5, before, -1.0)
    slot = lax.broadcasted_iota(jnp.int32, (experts, capacity, rows), 1).astype(f32)
    dispatch = (held[:, None, :] == slot).astype(f32).reshape(slots, rows)
    dispatch_ref[...] = dispatch.astype(bf16)
    combine_ref[...] = dispatch.T.astype(bf16)
    here = lax.axis_index("expert")
    weight = jnp.sum(jnp.where(ids == here, gw_ref[...], 0.0), axis=0, keepdims=True)
    mine = jnp.sum(jnp.where(expert == here, held, 0.0), axis=0, keepdims=True)
    slot = lax.broadcasted_iota(jnp.int32, (capacity, rows), 0).astype(f32)
    weight = jnp.sum(jnp.where(mine == slot, weight, 0.0), axis=1, keepdims=True)
    weight_ref[...] = jnp.broadcast_to(weight, weight_ref.shape)
    width = residual_ref.shape[1]
    residual_out[...] = jnp.concatenate(
        [residual_ref[...].astype(f32), jnp.zeros((rows, LANES - width), f32)], axis=1
    )
    gain = jnp.concatenate(
        [gain_ref[...].astype(f32), jnp.zeros((1, LANES - width), f32)], axis=1
    )
    gain_out[...] = jnp.broadcast_to(gain, gain_out.shape)
    for copy in copies[-2:]:
        copy.wait()
    o_out[...] = o_ref[...]


def values_body(parts_ref, uv_ref, out_ref):
    parts = parts_ref[...].astype(f32)
    heads = parts.shape[1]
    stats = parts[:, :, LAT:]
    scale = stats[:, :, 0:1] + stats[:, :, 1:2]
    total = stats[:, :, 2:3] + stats[:, :, 3:4]
    factor = jnp.exp(scale - jnp.max(scale, axis=0, keepdims=True))
    denominator = jnp.sum(factor * total, axis=0)
    attended = jnp.sum(factor * parts[:, :, :LAT], axis=0) / denominator
    row = lax.broadcasted_iota(jnp.int32, attended.shape, 0)
    spread = jnp.concatenate(
        [jnp.where(row == j, attended, 0.0).astype(bf16) for j in range(heads)], axis=1
    )
    head_vals = jnp.dot(spread, uv_ref[...], preferred_element_type=f32).astype(bf16)
    out_ref[...] = jnp.broadcast_to(head_vals[None], out_ref.shape)


def project_body(vals_ref, o_ref, out_ref):
    order = ring("expert", vals_ref.shape[0])
    vals = jnp.stack([vals_ref[order.index(i)] for i in range(len(order))]).astype(f32)
    wide = jnp.concatenate([vals[:, j, :] for j in range(vals.shape[1])], axis=1).astype(bf16)
    part = lax.dot_general(
        wide, o_ref[...], (((1,), (1,)), ((), ())), preferred_element_type=f32
    ).astype(bf16)
    part = jnp.concatenate(
        [part, jnp.zeros((part.shape[0], LANES - part.shape[1]), bf16)], axis=1
    )
    out_ref[...] = jnp.broadcast_to(part[None], out_ref.shape)


def mix_body(width, parts_ref, residual_ref, gain_ref, dispatch_ref, out_ref, mixed_ref):
    attn = jnp.sum(parts_ref[...].astype(f32), axis=0)
    mixed = (residual_ref[...] + attn).astype(bf16).astype(f32)
    mixed_ref[...] = mixed
    squares = jnp.sum(mixed * mixed, axis=1, keepdims=True)
    top = squares.astype(bf16).astype(f32)
    lane = lax.broadcasted_iota(jnp.int32, mixed.shape, 1)
    scaled = jnp.where(
        lane == width, top, jnp.where(lane == width + 1, squares - top, mixed * gain_ref[0:1])
    )
    slots = jnp.dot(dispatch_ref[...], scaled.astype(bf16), preferred_element_type=f32)
    slots = slots.astype(bf16).reshape(out_ref.shape)
    for i, expert in enumerate(ring("expert", out_ref.shape[0])):
        out_ref[i] = slots[expert]


def expert_body(slots_ref, gate_ref, up_ref, down_ref, weight_ref, out_ref):
    owners, capacity = slots_ref.shape[:2]
    features, units = gate_ref.shape
    width = features // owners
    lane = lax.broadcasted_iota(jnp.int32, (capacity, LANES), 1)
    stats = jnp.sum(slots_ref[...].astype(f32), axis=0)
    stats = jnp.where((lane == width) | (lane == width + 1), stats, 0.0)
    scale = lax.rsqrt(jnp.sum(stats, axis=1, keepdims=True) / features + norm_eps)
    order = ring("expert", owners)
    wide = jnp.concatenate(
        [slots_ref[order.index(i)][:, :width] for i in range(owners)], axis=1
    )
    gate_act = jnp.dot(wide, gate_ref[...], preferred_element_type=f32) * scale
    up_act = jnp.dot(wide, up_ref[...], preferred_element_type=f32) * scale
    hidden = (gate_act / (1.0 + jnp.exp(-gate_act)) * up_act).astype(bf16)
    outcome = jnp.dot(hidden, down_ref[...], preferred_element_type=f32) * weight_ref[:, 0:1]
    pad = jnp.zeros((capacity, LANES - width), f32)
    for i, owner in enumerate(order):
        out_ref[i] = jnp.concatenate(
            [outcome[:, owner * width : (owner + 1) * width], pad], axis=1
        ).astype(bf16)


def gather_body(parts_ref, combine_ref, mixed_ref, out_ref):
    order = ring("expert", parts_ref.shape[0])
    parts = jnp.stack([parts_ref[order.index(i)] for i in range(len(order))])
    parts = parts.reshape(combine_ref.shape[1], LANES)
    share = jnp.dot(combine_ref[...], parts, preferred_element_type=f32)
    share = share + jnp.where(lax.axis_index("head") == 0, mixed_ref[...], 0.0)
    groups, rows = out_ref.shape[0], share.shape[0]
    for i, owner in enumerate(ring("head", groups)):
        out_ref[i] = share[owner * rows // groups : (owner + 1) * rows // groups]


def finish_body(parts_ref, out_ref):
    columns = out_ref.shape[1]
    out_ref[...] = jnp.sum(parts_ref[...], axis=0)[:, :columns].astype(bf16)


def local(
    queries,
    kv_cache,
    block_ids,
    w_uv,
    o_proj,
    residual,
    moe_gain,
    w_gate,
    w_up,
    w_down,
    expert_ids,
    gate_weights,
):
    head_n = lax.axis_size("head")
    expert_n = lax.axis_size("expert")
    heads, width = queries.shape[1:]
    rows, top = expert_ids.shape
    columns = o_proj.shape[1]
    row_share = rows // head_n
    capacity = min(2 * (rows // expert_n) * top, rows)
    slots = expert_n * capacity

    tokens = kv_cache.shape[1]
    chips = head_n // 2
    alike = [[(head_n // 2 + 2 + 2 * i + core) % head_n for i in range(chips)] for core in (0, 1)]
    other = lax.ppermute(kv_cache[0].T, "head", [(i, i ^ 1) for i in range(head_n)])
    staged = pl.pallas_call(
        stage_body,
        out_shape=(
            shape((chips, heads, width), bf16),
            shape((slots, rows), bf16),
            shape((rows, slots), bf16),
            shape((capacity, LANES), f32),
            shape((rows, LANES), f32),
            shape((8, LANES), f32),
            shape((8, 2 * tokens), f32),
            shape(o_proj.shape[::-1], bf16),
            shape((width, tokens), bf16),
        ),
        in_specs=[pl.BlockSpec(memory_space=pltpu.HBM)] * 8,
        out_specs=(VM,) * 9,
        scratch_shapes=[
            pltpu.VMEM(queries.shape, bf16),
            pltpu.VMEM((top, rows), jnp.int32),
            pltpu.VMEM((top, rows), f32),
            pltpu.VMEM((rows, columns), bf16),
            pltpu.VMEM((1, columns), bf16),
            pltpu.VMEM(block_ids.shape, jnp.int32),
            pltpu.VMEM((columns, o_proj.shape[0]), bf16),
            pltpu.SemaphoreType.DMA((8,)),
        ],
        compiler_params=pltpu.CompilerParams(vmem_limit_bytes=48 * 1024 * 1024),
    )(
        *(
            pltpu.with_memory_space_constraint(array, pltpu.HBM)
            for array in (
                queries,
                expert_ids.T,
                gate_weights.T,
                residual,
                moe_gain[None, :],
                block_ids,
                o_proj.T,
                kv_cache[0].T,
            )
        )
    )
    asked, dispatch, combine, weight, residual_wide, gain, chosen, o_proj, cache = staged
    asked = exchange(asked, "head", alike)
    shares = call(
        attend_body,
        shape((chips * heads, LAT + LANES), bf16),
        [VM] * 4,
        chosen,
        asked.reshape(chips * heads, width),
        cache,
        other,
    )
    shares = exchange(shares.reshape(chips, heads, LAT + LANES), "head", alike)
    vals = call(
        values_body,
        shape((expert_n, heads, w_uv.shape[2]), bf16),
        [VM, VM],
        shares,
        w_uv.reshape(heads * LAT, -1),
    )
    vals = exchange(vals, "expert")
    attn = call(project_body, shape((head_n, rows, LANES), bf16), [VM, VM], vals, o_proj)
    attn = exchange(attn, "head")
    tokens, mixed = call(
        functools.partial(mix_body, columns),
        (shape((expert_n, capacity, LANES), bf16), shape((rows, LANES), f32)),
        [VM] * 4,
        attn,
        residual_wide,
        gain,
        dispatch,
    )
    tokens = exchange(tokens, "expert")
    outcome = call(
        expert_body,
        shape((expert_n, capacity, LANES), bf16),
        [VM] * 5,
        tokens,
        w_gate[0],
        w_up[0],
        w_down[0],
        weight,
    )
    outcome = exchange(outcome, "expert")
    moe = call(gather_body, shape((head_n, row_share, LANES), f32), [VM] * 3, outcome, combine, mixed)
    return call(finish_body, shape((row_share, columns), bf16), [VM], exchange(moe, "head"))


def solution(mesh):
    in_specs = (
        P("expert", "head", None),
        P("expert", "head", None),
        P("expert", None),
        P("head", None, None),
        P("head", "expert"),
        P(None, "expert"),
        P("expert"),
        P("expert", None, "head"),
        P("expert", None, "head"),
        P("expert", "head", None),
        P(),
        P(),
    )
    out_specs = P("head", "expert")
    return jax.shard_map(local, mesh=mesh, in_specs=in_specs, out_specs=out_specs, check_vma=False)
```
